128 devices in a mesh: lev: 4 (over x), sub: 32 (over z, y, core).
Axes of the slice: x: 4, y: 4, z: 4, core: 2. Of those that a mesh axis runs over, the one named last changes fastest.
Arguments:
- length_x: float32 [32, 128], P('lev', 'sub'), may hold values from 2 to 200
- length_y: float32 [3072, 32], P(('lev', 'sub')), may hold values from 2 to 128
- length_z: float32 [3072, 128], P(('lev', 'sub')), may hold values from 1 to 32
- sigma: float32 [3072, 32, 128], P(('lev', 'sub')), may hold values from 0.3 to 3
- obs_profile: bfloat16 [32, 1048576], P(None, ('lev', 'sub')), may hold values from -1 to 1
- obs_scale: float32 [1048576], P(('lev', 'sub')), may hold values from 0.3 to 3
- innovation: bfloat16 [1048576], P(('lev', 'sub')), may hold values from -6 to 6
- obs_column: int32 [1048576], P(('lev', 'sub')), may hold values from 0 to 393215, as said below
- obs_count: int32 [128, 128], replicated, may hold values from 1 to 64, as said below
Outputs:
- control: float32 [32, 128, 3072], P('lev', 'sub')
- increment: float32 [3072, 32, 128], P(('lev', 'sub'))
- departures: float32 [1048576], P(('lev', 'sub'))
The draws below stay inside these ranges and needn't reach their ends.
Inputs may be any that keep to these rules, and one draw needn't show every extreme that they name: `obs_column`: slot o names a column whose x lies among the 24 columns numbered from ((o // 64) % 128) * 24. `obs_count`: every sending device has a block with all 64 slots live, and one owner receives full blocks from every device.
All inputs are finite; a program needn't handle non-finite values.
Results may differ from the reference program's by a relative error of at most 0.0029.
Values may be sent and summed in bfloat16 or wider, within the bound.
A program may use at most 128 MiB of HBM per device.

```python
import math
import jax
import jax.numpy as jnp
from jax import lax

CAP = 64
NX = 3072
ITERS = 2
LEV = 32
NY = 128
BLOCKS = 128
NXB = 24
NOBS = 1048576
N_LEV = 4
N_SUB = 32


def draw_obs_column(key, part):
    key = jax.random.fold_in(key, 11)
    first_key, second_key = jax.random.split(key)
    slot_index = jnp.arange(NOBS, dtype=jnp.int32)
    owner_block = slot_index // CAP % BLOCKS
    grid_row = jax.random.randint(first_key, (NOBS,), 0, NY, dtype=jnp.int32)
    grid_col = jax.random.randint(second_key, (NOBS,), 0, NXB, dtype=jnp.int32)
    return grid_row * NX + owner_block * NXB + grid_col


def draw_obs_count(key, part):
    key = jax.random.fold_in(key, 23)
    keys = jax.random.split(key, 4)
    upper = max(1, CAP // 4) + 1
    base_count = jax.random.randint(keys[0], (BLOCKS, BLOCKS), 1, upper, dtype=jnp.int32)
    heavy = jax.random.randint(keys[1], (BLOCKS,), 1, 5, dtype=jnp.int32)
    counted = jnp.minimum(base_count * heavy[None, :], CAP)
    full_target = jax.random.randint(keys[2], (BLOCKS,), 0, BLOCKS, dtype=jnp.int32)
    busy_owner = jax.random.randint(keys[3], (), 0, BLOCKS, dtype=jnp.int32)
    owners = jnp.arange(BLOCKS, dtype=jnp.int32)
    full_block = (owners[None, :] == full_target[:, None]) | (owners[None, :] == busy_owner)
    return jnp.where(full_block, CAP, counted).astype(jnp.int32)


def shard_levels(key, shape, cuts, smallest, high):
    def one(position, parts):
        heights = jax.random.uniform(jax.random.fold_in(jax.random.fold_in(key, 6), position), (parts,), jnp.float32, smallest / len(cuts), high / len(cuts))
        return jnp.repeat(jnp.exp(heights), shape[position] // parts).reshape((-1,) + (1,) * (len(shape) - position - 1))

    loudness = one(*cuts[0])
    for cut in cuts[1:]:
        loudness = loudness * one(*cut)
    return loudness


def noise(rng, extent, width, limit, pieces=(), kind=jnp.bfloat16):
    entries = jax.random.normal(rng, extent, jnp.float32) * width
    if len(pieces) > 0:
        entries = shard_levels(rng, extent, pieces, -0.22, 0.18) * entries
    return jnp.clip(entries, min=-limit, max=limit).astype(kind)


def setup_inputs(seed: int = 0) -> dict:
    streams_of = jax.random.split(jax.random.key(seed), 10)
    length_x = jnp.clip(jnp.exp(math.log(200.0) - 4.6051702 * jax.random.uniform(streams_of[0], (LEV, NY), jnp.float32) ** shard_levels(streams_of[0], (LEV, NY), ((0, 4), (1, 32)), -0.2, 0.2)), 2.0, 200.0)
    length_y = jnp.clip(jnp.exp(math.log(128.0) - 4.158883 * jax.random.uniform(streams_of[1], (NX, LEV), jnp.float32) ** shard_levels(streams_of[1], (NX, LEV), ((0, 128),), -0.2, 0.2)), 2.0, 128.0)
    length_z = jnp.clip(jnp.exp(math.log(32.0) - 3.465736 * jax.random.uniform(streams_of[2], (NX, NY), jnp.float32) ** shard_levels(streams_of[2], (NX, NY), ((0, 128),), -0.2, 0.2)), 1.0, 32.0)
    sigma = jnp.clip(jnp.exp(math.log(3.0) - 2.3025851 * jax.random.uniform(streams_of[3], (NX, LEV, NY), jnp.float32) ** shard_levels(streams_of[3], (NX, LEV, NY), ((0, 128),), -0.2, 0.2)), 0.3, 3.0)
    obs_profile = noise(streams_of[4], (LEV, NOBS), LEV ** -0.5, 1.0, ((1, 128),))
    obs_scale = jnp.clip(jnp.exp(math.log(3.0) - 2.3025851 * jax.random.uniform(streams_of[5], (NOBS,), jnp.float32) ** shard_levels(streams_of[5], (NOBS,), ((0, 128),), -0.2, 0.2)), 0.3, 3.0)
    innovation = noise(streams_of[6], (NOBS,), 1.0, 6.0, ((0, 128),))
    obs_column = draw_obs_column(jax.random.fold_in(streams_of[9], 71), 0)
    obs_count = draw_obs_count(jax.random.fold_in(streams_of[9], 71), 0)
    return dict(length_x=length_x, length_y=length_y, length_z=length_z, sigma=sigma, obs_profile=obs_profile, obs_scale=obs_scale, innovation=innovation, obs_column=obs_column, obs_count=obs_count)


def coefficients(length):
    decay = jnp.exp(-1.0 / length)
    square = decay * decay
    gain = jnp.power(1.0 - square, 0.75) / jnp.power(1.0 + square, 0.25)
    return decay, gain


def recursion(field, decay, gain, axis):
    def combine(earlier, later):
        return (earlier[0] * later[0], later[0] * earlier[1] + later[1])

    factor = jnp.broadcast_to(decay, field.shape)
    return lax.associative_scan(combine, (factor, gain * field), axis=axis)[1]


def smooth(field, pair, axis):
    decay, gain = pair
    onward = recursion(field, decay, gain, axis)
    return jnp.flip(recursion(jnp.flip(onward, axis), decay, gain, axis), axis)


def reference(length_x, length_y, length_z, sigma, obs_profile, obs_scale, innovation, obs_column, obs_count):
    pair_x = coefficients(length_x[None, :, :])
    pair_y = coefficients(length_y[:, :, None])
    pair_z = coefficients(length_z[:, None, :])

    def forward_u(field):
        return sigma * smooth(smooth(smooth(field, pair_x, 0), pair_y, 2), pair_z, 1)

    def adjoint_u(field):
        return smooth(smooth(smooth(sigma * field, pair_z, 1), pair_y, 2), pair_x, 0)

    slots = jnp.arange(CAP, dtype=jnp.int32)
    live_mask = (slots[None, None, :] < obs_count[:, :, None]).astype(jnp.float32).reshape(NOBS)
    rounded = lax.optimization_barrier((obs_scale[None, :] * obs_profile.astype(jnp.float32)).astype(jnp.bfloat16))
    weights = rounded.astype(jnp.float32)
    innov = live_mask * innovation.astype(jnp.float32)
    col_index = (obs_column % NX).astype(jnp.int32)
    row_index = (obs_column // NX).astype(jnp.int32)

    def observe(field):
        values = field[col_index, :, row_index]
        return live_mask * jnp.sum(weights * values.T, axis=0)

    def spread(values):
        total = jnp.zeros((NX, LEV, NY), jnp.float32)
        return total.at[col_index, :, row_index].add((weights * values[None, :]).T)

    rhs = adjoint_u(spread(innov))
    control = jnp.zeros((NX, LEV, NY), jnp.float32)
    increment = jnp.zeros((NX, LEV, NY), jnp.float32)
    hinc = jnp.zeros((NOBS,), jnp.float32)
    residual = rhs
    direction = rhs
    norm_now = jnp.sum(residual * residual)
    for step in range(ITERS):
        image_u = forward_u(direction)
        image_obs = observe(image_u)
        image = direction + adjoint_u(spread(image_obs))
        alpha = norm_now / jnp.sum(direction * image)
        control = control + alpha * direction
        increment = increment + alpha * image_u
        hinc = hinc + alpha * image_obs
        residual = residual - alpha * image
        norm_next = jnp.sum(residual * residual)
        direction = residual + (norm_next / norm_now) * direction
        norm_now = norm_next
    blocks = N_LEV * N_SUB
    anchor_order = hinc - innov
    departures = anchor_order.reshape(blocks, blocks, CAP).transpose(1, 0, 2).reshape(NOBS)
    return control.transpose(1, 2, 0), increment, departures
```

```python
import functools

import jax
import jax.numpy as jnp
from jax import lax
from jax.experimental import pallas as pl
from jax.experimental.pallas import tpu as pltpu
from jax.sharding import PartitionSpec as P

MESH = pl.DeviceIdType.MESH
F32 = jnp.float32
BF16 = jnp.bfloat16
NLEV = 4
NSUB = 32
NDEV = NLEV * NSUB
NXB = 24
LEV = 32
NY = 128
CAP = 64
CELLS = NXB * LEV
NOBS = NDEV * CAP
HALF = NXB // 2
WROWS = HALF * LEV
TILES = NOBS // 128


def gain_of(decay):
    square = decay * decay
    below = jnp.sqrt(1.0 - square)
    return below * jnp.sqrt(below) / jnp.sqrt(jnp.sqrt(1.0 + square))


def chunked_loop(count, unroll, body):
    def step(i, carry):
        for k in range(unroll):
            body(i * unroll + k)
        return carry

    lax.fori_loop(0, count // unroll, step, 0)


def split(value):
    high = value.astype(BF16)
    return high, (value - high.astype(F32)).astype(BF16)


def kernel(
    prof_ref, scale_ref, meta_ref, sigma_ref, ly_ref, lz_ref,
    control_ref, increment_ref, dep_ref,
    ws, wl, ml, wide, rowhot, innov_ref, lenx_ref, dec_ref, gain_ref, resp_ref,
    pw, gy_ref, v, ubuf, x0, y0, x1, y1, tacc, fth, ftl, zs,
    es, el, cs, cr, cl, sc_src, sc_land,
    obs_send, obs_recv, edge_send, edge_recv, back_send, back_recv, sc_send, sc_recv,
):
    lev_i = lax.axis_index("lev")
    sub_i = lax.axis_index("sub")
    me = lev_i * NSUB + sub_i

    def device(index):
        return (index // NSUB, lax.rem(index, NSUB))

    def other(k):
        return lax.rem(me + k, NDEV)

    barrier = pltpu.get_barrier_semaphore()

    def greet(k, carry):
        pl.semaphore_signal(barrier, inc=1, device_id=device(other(k)), device_id_type=MESH)
        return carry

    lax.fori_loop(1, NDEV, greet, 0)

    lane = lax.broadcasted_iota(jnp.int32, (1, 128), 1)
    low_half = lane < CAP

    def pack(i, carry):
        at = pl.ds(pl.multiple_of(i * 128, 128), 128)
        w = prof_ref[:, at].astype(F32) * scale_ref[:, at]
        top, bottom = w[:16], w[16:]
        ws[2 * i] = jnp.where(low_half, top, pltpu.roll(bottom, CAP, 1)).astype(BF16)
        ws[2 * i + 1] = jnp.where(low_half, pltpu.roll(top, CAP, 1), bottom).astype(BF16)
        return carry

    lax.fori_loop(0, TILES, pack, 0)
    pl.semaphore_wait(barrier, NDEV - 1)

    def send_obs(k, carry):
        to = other(k)
        pltpu.make_async_remote_copy(
            src_ref=meta_ref.at[to], dst_ref=ml.at[me], send_sem=obs_send.at[0],
            recv_sem=obs_recv.at[0], device_id=device(to), device_id_type=MESH,
        ).start()
        pltpu.make_async_remote_copy(
            src_ref=ws.at[to], dst_ref=wl.at[me], send_sem=obs_send.at[1],
            recv_sem=obs_recv.at[1], device_id=device(to), device_id_type=MESH,
        ).start()
        return carry

    lax.fori_loop(1, NDEV, send_obs, 0)
    ml[me] = meta_ref[me]
    wl[me] = ws[me]

    decay_y = jnp.exp(-1.0 / ly_ref[...])
    gy_ref[...] = jnp.broadcast_to(gain_of(decay_y), (CELLS, 128))
    power = decay_y
    for k in range(7):
        pw[k] = jnp.broadcast_to(power, (CELLS, 128))
        power = power * power
    decay_z = jnp.exp(-1.0 / lz_ref[...])
    gain_z = gain_of(decay_z)

    def wait_all(src, dst, send_sem, recv_sem):
        copy = pltpu.make_async_remote_copy(
            src_ref=src, dst_ref=dst, send_sem=send_sem, recv_sem=recv_sem,
            device_id=(lev_i, sub_i), device_id_type=MESH,
        )
        copy.wait_recv()
        copy.wait_send()

    rest = pl.ds(0, NDEV - 1)
    wait_all(meta_ref.at[rest], ml.at[rest], obs_send.at[0], obs_recv.at[0])

    lengths = ml[:, 1, :]
    k_id = lax.broadcasted_iota(jnp.int32, (128, 128), 0)
    y_id = lax.broadcasted_iota(jnp.int32, (128, 128), 1)
    mine = (lax.rem(k_id, NSUB) == y_id // 4).astype(F32)
    for row in range(8):
        pick = (k_id == row * 4 + lax.rem(y_id, 4)).astype(F32)
        spread_row = jnp.dot(
            lengths, pick, precision=lax.Precision.HIGHEST, preferred_element_type=F32
        )
        rows = jnp.sum((spread_row * mine).reshape(NLEV, NSUB, 128), axis=1)
        lenx_ref[pl.ds(row, NLEV, stride=8), :] = rows
    decay_x = jnp.exp(-1.0 / lenx_ref[...])
    gain_x = gain_of(decay_x)
    dec_ref[...] = decay_x
    gain_ref[...] = gain_x

    level = pl.ds(sub_i, 1)
    a = dec_ref[level, :]
    g = gain_ref[level, :]
    up = [a]
    for _ in range(NXB - 1):
        up.append(up[-1] * a)

    def sweep(values):
        total = jnp.zeros_like(a)
        out = []
        for value in values:
            total = a * total + g * value
            out.append(total)
        return out

    block_decay = up[-1]
    p1 = sweep(up[::-1])[::-1]
    q1 = sweep(p1)
    q2 = sweep(up[::-1])
    r1 = sweep(q1[::-1])
    r2 = sweep(q2[::-1])
    for index, value in enumerate((block_decay, p1[0], q1[-1], q2[-1], r1[-1], r2[-1])):
        resp_ref[pl.ds(index, 1), :] = value

    wait_all(ws.at[rest], wl.at[rest], obs_send.at[1], obs_recv.at[1])

    place = lax.broadcasted_iota(jnp.int32, (256, 128), 0)

    def widen(i, carry):
        at = pl.ds(pl.multiple_of(i * 128, 128), 128)
        even, odd = wl[2 * i].astype(F32), wl[2 * i + 1].astype(F32)
        low = jnp.where(low_half, even, pltpu.roll(odd, CAP, 1))
        high = jnp.where(low_half, pltpu.roll(even, CAP, 1), odd)
        w = jnp.concatenate([low, high], axis=0)
        m_even, m_odd = ml[2 * i, pl.ds(0, 1), :], ml[2 * i + 1, pl.ds(0, 1), :]
        innov_ref[:, at] = jnp.where(low_half, m_even, pltpu.roll(m_odd, CAP, 1))
        key = jnp.where(low_half, pltpu.roll(m_even, CAP, 1), m_odd).astype(jnp.int32)
        spot = key // 16
        column = key - 16 * spot
        for c in range(HALF):
            wide[pl.ds(c * LEV, LEV), at] = jnp.where(column == c, w, 0.0).astype(BF16)
        rowhot[:, at] = jnp.where(place == spot, 1.0, 0.0).astype(BF16)
        return carry

    lax.fori_loop(0, TILES, widen, 0)

    CHUNK = 1024

    def spread(source, exact):
        tacc[...] = jnp.zeros_like(tacc)

        def step(i, carry):
            at = pl.ds(pl.multiple_of(i * CHUNK, CHUNK), CHUNK)
            hot = rowhot[:, at]
            parts = split(source[:, at])
            if exact:
                parts = parts[:1]
            total = tacc[...]
            for part in parts:
                total += lax.dot_general(
                    wide[:, at], hot * part, (((1,), (1,)), ((), ())),
                    preferred_element_type=F32,
                )
            tacc[...] = total
            return carry

        lax.fori_loop(0, NOBS // CHUNK, step, 0)

    def observe(field, out):
        side = jnp.concatenate([field[pl.ds(0, WROWS), :], field[pl.ds(WROWS, WROWS), :]], axis=1)
        fth[...], ftl[...] = split(side.T)

        def step(i, carry):
            at = pl.ds(pl.multiple_of(i * CHUNK, CHUNK), CHUNK)
            w = wide[:, at]
            got = jnp.dot(fth[...], w, preferred_element_type=F32)
            got += jnp.dot(ftl[...], w, preferred_element_type=F32)
            out[:, at] = jnp.sum(got * rowhot[:, at].astype(F32), axis=0, keepdims=True)
            return carry

        lax.fori_loop(0, NOBS // CHUNK, step, 0)

    def filter_z(ref):
        def row(z):
            return pl.ds(z, NXB, stride=LEV)

        def onward(i, total):
            for k in range(8):
                z = i * 8 + k
                total = decay_z * total + gain_z * ref[row(z), :]
                ref[row(z), :] = total
            return total

        def backward(i, total):
            for k in range(8):
                z = LEV - 1 - (i * 8 + k)
                total = decay_z * total + gain_z * ref[row(z), :]
                ref[row(z), :] = total
            return total

        lax.fori_loop(0, LEV // 8, onward, jnp.zeros((NXB, 128), F32))
        lax.fori_loop(0, LEV // 8, backward, jnp.zeros((NXB, 128), F32))

    YROWS = 128

    def filter_y(ref):
        def step(i, carry):
            at = pl.ds(pl.multiple_of(i * YROWS, YROWS), YROWS)
            gain = gy_ref[at, :]
            value = gain * ref[at, :]
            for k in range(7):
                moved = jnp.where(lane >= (1 << k), pltpu.roll(value, 1 << k, 1), 0.0)
                value = value + pw[k, at, :] * moved
            value = gain * value
            for k in range(7):
                moved = jnp.where(
                    lane < 128 - (1 << k), pltpu.roll(value, 128 - (1 << k), 1), 0.0
                )
                value = value + pw[k, at, :] * moved
            ref[at, :] = value
            return carry

        lax.fori_loop(0, CELLS // YROWS, step, 0)

    def sweep_x(src, dst, start, reverse):
        decay, gain = dec_ref[...], gain_ref[...]

        def step(i, total):
            for k in range(6):
                c = i * 6 + k
                if reverse:
                    c = NXB - 1 - c
                at = pl.ds(pl.multiple_of(c * LEV, LEV), LEV)
                total = decay * total + gain * src[at, :]
                dst[at, :] = total
            return total

        return lax.fori_loop(0, NXB // 6, step, start)

    def scan(values, reverse):
        sub = lax.broadcasted_iota(jnp.int32, (NDEV, 1), 0)
        factor = resp_ref[pl.ds(0, 1), :]
        for k in range(7):
            d = 1 << k
            if reverse:
                moved = jnp.where(sub < NDEV - d, pltpu.roll(values, NDEV - d, 0), 0.0)
            else:
                moved = jnp.where(sub >= d, pltpu.roll(values, d, 0), 0.0)
            values = values + factor * moved
            factor = factor * factor
        if reverse:
            return jnp.where(sub < NDEV - 1, pltpu.roll(values, NDEV - 1, 0), 0.0)
        return jnp.where(sub >= 1, pltpu.roll(values, 1, 0), 0.0)

    def covariance(turn, x_out, y_out):
        v[pl.ds(0, WROWS), :] = tacc[:, pl.ds(0, 128)] * sigma_ref[pl.ds(0, WROWS), :]
        v[pl.ds(WROWS, WROWS), :] = tacc[:, pl.ds(128, 128)] * sigma_ref[pl.ds(WROWS, WROWS), :]
        filter_z(v)
        filter_y(v)
        zero = jnp.zeros((LEV, 128), F32)
        es[:, 0, :] = sweep_x(v, ubuf, zero, False)
        es[:, 1, :] = sweep_x(ubuf, ubuf, zero, True)
        es[:, 2, :] = sweep_x(ubuf, ubuf, zero, False)
        es[:, 3, :] = sweep_x(ubuf, ubuf, zero, True)

        def send_edges(k, carry):
            to = other(k)
            pltpu.make_async_remote_copy(
                src_ref=es.at[lax.rem(to, NSUB)], dst_ref=el.at[turn, me],
                send_sem=edge_send.at[turn], recv_sem=edge_recv.at[turn],
                device_id=device(to), device_id_type=MESH,
            ).start()
            return carry

        lax.fori_loop(1, NDEV, send_edges, 0)
        el[turn, me] = es[sub_i]
        wait_all(el.at[turn, rest], el.at[turn, rest], edge_send.at[turn], edge_recv.at[turn])

        e1, e2 = el[turn, :, 0, :], el[turn, :, 1, :]
        e3, e4 = el[turn, :, 2, :], el[turn, :, 3, :]
        _, k1, k2, k3, k4, k5 = [resp_ref[pl.ds(i, 1), :] for i in range(6)]
        c1 = scan(e1, False)
        c2 = scan(e2 + k1 * c1, True)
        c3 = scan(e3 + k2 * c1 + k3 * c2, False)
        c4 = scan(e4 + k4 * c1 + k5 * c2 + k1 * c3, True)
        group = pl.ds(pl.multiple_of(lev_i * NSUB, NSUB), NSUB)
        for index, value in enumerate((c1, c2, c3, c4)):
            cs[...] = value
            cr[:, index, :] = cs[group, :]

        def send_back(k, carry):
            to = lax.rem(sub_i + k, NSUB)
            pltpu.make_async_remote_copy(
                src_ref=cr.at[to], dst_ref=cl.at[turn, sub_i],
                send_sem=back_send.at[turn], recv_sem=back_recv.at[turn],
                device_id=(lev_i, to), device_id_type=MESH,
            ).start()
            return carry

        lax.fori_loop(1, NSUB, send_back, 0)
        cl[turn, sub_i] = cr[sub_i]
        back = pl.ds(0, NSUB - 1)
        wait_all(cl.at[turn, back], cl.at[turn, back], back_send.at[turn], back_recv.at[turn])
        sweep_x(v, v, cl[turn, :, 0, :], False)
        sweep_x(v, x_out, cl[turn, :, 1, :], True)
        sweep_x(x_out, v, cl[turn, :, 2, :], False)
        sweep_x(v, y_out, cl[turn, :, 3, :], True)
        filter_y(y_out)
        filter_z(y_out)
        y_out[...] = y_out[...] * sigma_ref[...]

    def share(turn, sums):
        row = jnp.zeros((1, 128), F32)
        for index, value in enumerate(sums):
            row = jnp.where(lane == index, value, row)
        sc_src[turn] = row

        def go(k, carry):
            pltpu.make_async_remote_copy(
                src_ref=sc_src.at[turn], dst_ref=sc_land.at[turn, me],
                send_sem=sc_send.at[turn], recv_sem=sc_recv.at[turn],
                device_id=device(other(k)), device_id_type=MESH,
            ).start()
            return carry

        lax.fori_loop(1, NDEV, go, 0)
        sc_land[turn, me] = row

    def collect(turn, count):
        wait_all(
            sc_land.at[turn, rest], sc_land.at[turn, rest], sc_send.at[turn], sc_recv.at[turn]
        )
        total = jnp.sum(sc_land[turn, :, 0, :], axis=0, keepdims=True)
        return [
            jnp.sum(jnp.where(lane == index, total, 0.0), axis=1, keepdims=True)
            for index in range(count)
        ]

    def dot(left, right):
        return jnp.sum(jnp.sum(left * right, axis=0, keepdims=True), axis=1, keepdims=True)

    zrow0, zrow1 = zs.at[pl.ds(0, 1)], zs.at[pl.ds(1, 1)]
    spread(innov_ref, True)
    covariance(0, x0, y0)
    observe(y0, zrow0)
    z0 = zrow0[...]
    share(0, [dot(x0[...], x0[...]), dot(z0, z0)])
    spread(zrow0, False)
    covariance(1, x1, y1)
    rr0, zz0 = collect(0, 2)
    alpha0 = rr0 / (rr0 + zz0)
    x1[...] = (1.0 - alpha0) * x0[...] - alpha0 * x1[...]
    y1[...] = (1.0 - alpha0) * y0[...] - alpha0 * y1[...]
    observe(y1, zrow1)
    z1 = zrow1[...]
    share(1, [dot(x1[...], x1[...]), dot(x1[...], x0[...]), dot(z1, z1), dot(z1, z0)])
    rr1, cross, zz1, zcross = collect(1, 4)
    beta = rr1 / rr0
    curvature = rr1 + zz1 + 2.0 * beta * (cross + zcross) + beta * beta * (rr0 + zz0)
    alpha1 = rr1 / curvature
    old = alpha0 + alpha1 * beta
    control_ref[...] = old * x0[...] + alpha1 * x1[...]
    increment_ref[...] = old * y0[...] + alpha1 * y1[...]
    dep_ref[...] = old * z0 + alpha1 * z1 - innov_ref[...]


def body(
    length_x, length_y, length_z, sigma, obs_profile, obs_scale, innovation, obs_column, obs_count
):
    me = lax.axis_index(("lev", "sub"))
    width = NXB * NDEV
    counts = lax.dynamic_slice_in_dim(obs_count, me, 1, 0)[0]
    live = jnp.arange(CAP, dtype=jnp.int32)[None, :] < counts[:, None]
    scale = jnp.where(live, obs_scale.reshape(NDEV, CAP), 0.0).reshape(1, NOBS)
    innov = jnp.where(live, innovation.reshape(NDEV, CAP).astype(F32), 0.0)
    column = obs_column.reshape(NDEV, CAP)
    local = column % width - NXB * jnp.arange(NDEV, dtype=jnp.int32)[:, None]
    half = local // HALF
    spot = half * NY + column // width
    key = (spot * 16 + (local - HALF * half)).astype(F32)
    lengths = jnp.pad(length_x.reshape(1, 32), ((0, 0), (0, 96)))
    meta = jnp.stack(
        [jnp.concatenate([innov, key], axis=1), jnp.broadcast_to(lengths, (NDEV, 128))], axis=1
    )
    vmem = pl.BlockSpec(memory_space=pltpu.VMEM)
    field = pltpu.VMEM((CELLS, 128), F32)
    control, increment, departures = pl.pallas_call(
        kernel,
        out_shape=(
            jax.ShapeDtypeStruct((CELLS, 128), F32),
            jax.ShapeDtypeStruct((CELLS, 128), F32),
            jax.ShapeDtypeStruct((1, NOBS), F32),
        ),
        in_specs=[vmem] * 6,
        out_specs=(vmem,) * 3,
        scratch_shapes=[
            pltpu.VMEM((NDEV, 16, 128), BF16),
            pltpu.VMEM((NDEV, 16, 128), BF16),
            pltpu.VMEM((NDEV, 2, 128), F32),
            pltpu.VMEM((WROWS, NOBS), BF16),
            pltpu.VMEM((256, NOBS), BF16),
            pltpu.VMEM((1, NOBS), F32),
            pltpu.VMEM((LEV, 128), F32),
            pltpu.VMEM((LEV, 128), F32),
            pltpu.VMEM((LEV, 128), F32),
            pltpu.VMEM((8, 128), F32),
            pltpu.VMEM((7, CELLS, 128), F32),
            field,
            field,
            field,
            field,
            field,
            field,
            field,
            pltpu.VMEM((WROWS, 256), F32),
            pltpu.VMEM((256, WROWS), BF16),
            pltpu.VMEM((256, WROWS), BF16),
            pltpu.VMEM((2, NOBS), F32),
            pltpu.VMEM((LEV, 4, 128), F32),
            pltpu.VMEM((2, NDEV, 4, 128), F32),
            pltpu.VMEM((NDEV, 128), F32),
            pltpu.VMEM((NSUB, 4, 128), F32),
            pltpu.VMEM((2, LEV, 4, 128), F32),
            pltpu.VMEM((2, 1, 128), F32),
            pltpu.VMEM((2, NDEV, 1, 128), F32),
            pltpu.SemaphoreType.DMA((2,)),
            pltpu.SemaphoreType.DMA((2,)),
            pltpu.SemaphoreType.DMA((2,)),
            pltpu.SemaphoreType.DMA((2,)),
            pltpu.SemaphoreType.DMA((2,)),
            pltpu.SemaphoreType.DMA((2,)),
            pltpu.SemaphoreType.DMA((2,)),
            pltpu.SemaphoreType.DMA((2,)),
        ],
        compiler_params=pltpu.CompilerParams(
            collective_id=0, has_side_effects=True, vmem_limit_bytes=56 << 20
        ),
    )(
        obs_profile, scale, meta, sigma.reshape(CELLS, 128), length_y.reshape(CELLS, 1), length_z
    )
    pieces = control.reshape(NXB, NLEV, LEV // NLEV, NSUB, NY // NSUB).transpose(1, 3, 0, 2, 4)
    moved = lax.all_to_all(
        pieces.reshape(NDEV, -1), ("lev", "sub"), split_axis=0, concat_axis=0, tiled=True
    )
    rows = moved.reshape(NDEV, NXB, LEV // NLEV, NY // NSUB).transpose(2, 3, 0, 1)
    return (
        rows.reshape(LEV // NLEV, NY // NSUB, width),
        increment.reshape(NXB, LEV, NY),
        departures.reshape(NOBS),
    )


def solution(mesh):
    blocks = P(("lev", "sub"))
    placed = (
        P("lev", "sub"), blocks, blocks, blocks, P(None, ("lev", "sub")),
        blocks, blocks, blocks, P(),
    )
    return jax.shard_map(
        body,
        mesh=mesh,
        in_specs=placed,
        out_specs=(P("lev", "sub", None), blocks, blocks),
        check_vma=False,
    )
```

```python
import functools

import jax
import jax.numpy as jnp
from jax import lax
from jax.experimental import pallas as pl
from jax.experimental.pallas import tpu as pltpu
from jax.sharding import PartitionSpec as P

MESH = pl.DeviceIdType.MESH
F32 = jnp.float32
BF16 = jnp.bfloat16
NLEV = 4
NSUB = 32
NDEV = NLEV * NSUB
NXB = 24
LEV = 32
NY = 128
CAP = 64
CELLS = NXB * LEV
NOBS = NDEV * CAP
HALF = NXB // 2
WROWS = HALF * LEV
TILES = NOBS // 128
GROUPS = 4


def gain_of(decay):
    square = decay * decay
    below = jnp.sqrt(1.0 - square)
    return below * jnp.sqrt(below) / jnp.sqrt(jnp.sqrt(1.0 + square))


def chunked_loop(count, unroll, body):
    def step(i, carry):
        for k in range(unroll):
            body(i * unroll + k)
        return carry

    lax.fori_loop(0, count // unroll, step, 0)


def split(value):
    high = value.astype(BF16)
    return high, (value - high.astype(F32)).astype(BF16)


def kernel(
    lx_ref, ly_ref, lz_ref, sigma_ref, prof_ref, scale_ref, raw_ref, col_ref, count_ref,
    control_ref, increment_ref, dep_ref,
    live_ref, ms, ws, wl, ml, wide, rowhot, innov_ref, lenx_ref, dec_ref, gain_ref, resp_ref,
    pw, gy_ref, v, ubuf, vbuf, x0, y0, x1, y1, tacc, fth, ftl, zs,
    es, el, cs, cr, cl, sc_src, sc_land, tx1, ta, tx2, tb,
    meta_send, meta_recv, obs_send, obs_recv, edge_send, edge_recv, back_send, back_recv,
    sc_send, sc_recv, one_send, one_recv, two_send, two_recv,
):
    lev_i = lax.axis_index("lev")
    sub_i = lax.axis_index("sub")
    me = lev_i * NSUB + sub_i

    def device(index):
        return (index // NSUB, lax.rem(index, NSUB))

    def other(k):
        return lax.rem(me + k, NDEV)

    barrier = pltpu.get_barrier_semaphore()

    def greet(k, carry):
        pl.semaphore_signal(barrier, inc=1, device_id=device(other(k)), device_id_type=MESH)
        return carry

    lax.fori_loop(1, NDEV, greet, 0)

    lane = lax.broadcasted_iota(jnp.int32, (1, 128), 1)
    low_half = lane < CAP

    def wait_all(src, dst, send_sem, recv_sem):
        copy = pltpu.make_async_remote_copy(
            src_ref=src, dst_ref=dst, send_sem=send_sem, recv_sem=recv_sem,
            device_id=(lev_i, sub_i), device_id_type=MESH,
        )
        copy.wait_recv()
        copy.wait_send()

    rest = pl.ds(0, NDEV - 1)

    counts = jnp.broadcast_to(count_ref[pl.ds(me, 1), :], (TILES, 128))
    owner = lax.broadcasted_iota(jnp.int32, (TILES, 128), 1)
    tile = lax.broadcasted_iota(jnp.int32, (TILES, 128), 0)
    even_count = jnp.sum(jnp.where(owner == 2 * tile, counts, 0), axis=1, keepdims=True)
    odd_count = jnp.sum(jnp.where(owner == 2 * tile + 1, counts, 0), axis=1, keepdims=True)
    live = jnp.where(owner < CAP, owner, owner - CAP) < jnp.where(owner < CAP, even_count, odd_count)
    live_ref[...] = jnp.where(live, scale_ref[...], 0.0)
    innov_sent = jnp.where(live, raw_ref[...].astype(F32), 0.0)
    column = col_ref[...].astype(F32)
    row = jnp.floor((column + 0.5) * (1.0 / (NXB * NDEV)))
    first = (2 * tile + jnp.where(owner < CAP, 0, 1)) * NXB
    local = column - row * (NXB * NDEV) - first.astype(F32)
    half = jnp.where(local >= HALF, 1.0, 0.0)
    key_sent = (half * NY + row) * 16.0 + (local - HALF * half)
    even = jnp.where(low_half, innov_sent, pltpu.roll(key_sent, CAP, 1))
    odd = jnp.where(low_half, pltpu.roll(innov_sent, CAP, 1), key_sent)
    ms[:, 0, :] = jnp.stack([even, odd], axis=1).reshape(NDEV, 128)
    pick4 = (
        lax.broadcasted_iota(jnp.int32, (4, 128), 0)
        == lax.rem(lax.broadcasted_iota(jnp.int32, (4, 128), 1), 4)
    ).astype(F32)
    own = jnp.dot(
        lx_ref[...], pick4, precision=lax.Precision.HIGHEST, preferred_element_type=F32
    )
    own_at = lax.broadcasted_iota(jnp.int32, (8, 128), 1) // 4
    own = jnp.where(own_at == lax.broadcasted_iota(jnp.int32, (8, 128), 0), own, 0.0)
    ms[:, 1, :] = jnp.broadcast_to(jnp.sum(own, axis=0, keepdims=True), (NDEV, 128))

    def pack(i, carry):
        at = pl.ds(pl.multiple_of(i * 128, 128), 128)
        w = prof_ref[:, at].astype(F32) * live_ref[pl.ds(i, 1), :]
        top, bottom = w[:16], w[16:]
        ws[2 * i] = jnp.where(low_half, top, pltpu.roll(bottom, CAP, 1)).astype(BF16)
        ws[2 * i + 1] = jnp.where(low_half, pltpu.roll(top, CAP, 1), bottom).astype(BF16)
        return carry

    lax.fori_loop(0, TILES, pack, 0)
    pl.semaphore_wait(barrier, NDEV - 1)

    pair, core = me // 2, lax.rem(me, 2)
    PAIRS = TILES // GROUPS

    def send_block(kp, to_core):
        to_pair = lax.rem(pair + kp, TILES)
        to = 2 * to_pair + to_core
        group = kp // PAIRS
        pltpu.make_async_remote_copy(
            src_ref=ms.at[to], dst_ref=ml.at[me],
            send_sem=meta_send.at[group], recv_sem=meta_recv.at[group],
            device_id=device(to), device_id_type=MESH,
        ).start()
        pltpu.make_async_remote_copy(
            src_ref=ws.at[to], dst_ref=wl.at[me],
            send_sem=obs_send.at[group], recv_sem=obs_recv.at[group],
            device_id=device(to), device_id_type=MESH,
        ).start()

    send_block(0, 1 - core)

    def send_pair(kp, carry):
        send_block(kp, core)
        send_block(kp, 1 - core)
        return carry

    lax.fori_loop(1, TILES, send_pair, 0)
    ml[me] = ms[me]
    wl[me] = ws[me]

    decay_y = jnp.exp(-1.0 / ly_ref[...])
    gain_y = gain_of(decay_y).T
    decay_y = decay_y.T
    for c in range(NXB):
        rows = pl.ds(c * LEV, LEV)
        gy_ref[rows, :] = jnp.broadcast_to(gain_y[:, c:c + 1], (LEV, 128))
        power = jnp.broadcast_to(decay_y[:, c:c + 1], (LEV, 128))
        for k in range(7):
            pw[k, rows, :] = power
            power = power * power
    decay_z = jnp.exp(-1.0 / lz_ref[...])
    gain_z = gain_of(decay_z)

    place = lax.broadcasted_iota(jnp.int32, (256, 128), 0).astype(F32).astype(BF16)

    def widen(kp, carry):
        i = lax.rem(pair - kp + TILES, TILES)
        at = pl.ds(pl.multiple_of(i * 128, 128), 128)
        even, odd = wl[2 * i].astype(F32), wl[2 * i + 1].astype(F32)
        low = jnp.where(low_half, even, pltpu.roll(odd, CAP, 1))
        high = jnp.where(low_half, pltpu.roll(even, CAP, 1), odd)
        w = jnp.concatenate([low, high], axis=0).astype(BF16)
        m_even, m_odd = ml[2 * i, pl.ds(0, 1), :], ml[2 * i + 1, pl.ds(0, 1), :]
        innov_ref[:, at] = jnp.where(low_half, m_even, pltpu.roll(m_odd, CAP, 1))
        key = jnp.where(low_half, pltpu.roll(m_even, CAP, 1), m_odd)
        spot = jnp.floor(key * (1.0 / 16.0))
        column = jnp.broadcast_to(key - 16.0 * spot, (LEV, 128)).astype(BF16)
        for c in range(HALF):
            wide[pl.ds(c * LEV, LEV), at] = jnp.where(column == c, w, jnp.zeros_like(w))
        spot = jnp.broadcast_to(spot, (256, 128)).astype(BF16)
        rowhot[:, at] = jnp.where(place == spot, jnp.ones_like(place), jnp.zeros_like(place))
        return carry

    for group in range(GROUPS):
        blocks = pl.ds(0, 2 * PAIRS - (group == 0))
        wait_all(ms.at[blocks], ml.at[blocks], meta_send.at[group], meta_recv.at[group])
        wait_all(ws.at[blocks], wl.at[blocks], obs_send.at[group], obs_recv.at[group])
        lax.fori_loop(group * PAIRS, (group + 1) * PAIRS, widen, 0)

    lengths = ml[:, 1, :]
    k_id = lax.broadcasted_iota(jnp.int32, (128, 128), 0)
    y_id = lax.broadcasted_iota(jnp.int32, (128, 128), 1)
    mine = (lax.rem(k_id, NSUB) == y_id // 4).astype(F32)
    for row in range(8):
        pick = (k_id == row * 4 + lax.rem(y_id, 4)).astype(F32)
        spread_row = jnp.dot(
            lengths, pick, precision=lax.Precision.HIGHEST, preferred_element_type=F32
        )
        rows = jnp.sum((spread_row * mine).reshape(NLEV, NSUB, 128), axis=1)
        lenx_ref[pl.ds(row, NLEV, stride=8), :] = rows
    decay_x = jnp.exp(-1.0 / lenx_ref[...])
    gain_x = gain_of(decay_x)
    dec_ref[...] = decay_x
    gain_ref[...] = gain_x

    level = pl.ds(sub_i, 1)
    a = dec_ref[level, :]
    g = gain_ref[level, :]
    up = [a]
    for _ in range(NXB - 1):
        up.append(up[-1] * a)

    def sweep(values):
        total = jnp.zeros_like(a)
        out = []
        for value in values:
            total = a * total + g * value
            out.append(total)
        return out

    block_decay = up[-1]
    p1 = sweep(up[::-1])[::-1]
    q1 = sweep(p1)
    q2 = sweep(up[::-1])
    r1 = sweep(q1[::-1])
    r2 = sweep(q2[::-1])
    for index, value in enumerate((block_decay, p1[0], q1[-1], q2[-1], r1[-1], r2[-1])):
        resp_ref[pl.ds(index, 1), :] = value

    CHUNK = 2048

    def spread(source, exact):
        tacc[...] = jnp.zeros_like(tacc)

        def step(i, carry):
            at = pl.ds(pl.multiple_of(i * CHUNK, CHUNK), CHUNK)
            hot = rowhot[:, at]
            parts = split(source[:, at])
            if exact:
                parts = parts[:1]
            total = tacc[...]
            for part in parts:
                total += lax.dot_general(
                    wide[:, at], hot * part, (((1,), (1,)), ((), ())),
                    preferred_element_type=F32,
                )
            tacc[...] = total
            return carry

        lax.fori_loop(0, NOBS // CHUNK, step, 0)

    def observe(field, out):
        side = jnp.concatenate([field[pl.ds(0, WROWS), :], field[pl.ds(WROWS, WROWS), :]], axis=1)
        fth[...], ftl[...] = split(side.T)

        def step(i, carry):
            at = pl.ds(pl.multiple_of(i * CHUNK, CHUNK), CHUNK)
            w = wide[:, at]
            got = jnp.dot(fth[...], w, preferred_element_type=F32)
            got += jnp.dot(ftl[...], w, preferred_element_type=F32)
            out[:, at] = jnp.sum(got * rowhot[:, at].astype(F32), axis=0, keepdims=True)
            return carry

        lax.fori_loop(0, NOBS // CHUNK, step, 0)

    def filter_z(src, mid, dst):
        def row(z):
            return pl.ds(z, NXB, stride=LEV)

        total = jnp.zeros((NXB, 128), F32)
        for z in range(LEV):
            total = decay_z * total + gain_z * src[row(z), :]
            mid[row(z), :] = total
        total = jnp.zeros((NXB, 128), F32)
        for z in range(LEV - 1, -1, -1):
            total = decay_z * total + gain_z * mid[row(z), :]
            dst[row(z), :] = total

    def filter_y(src, dst):
        gain = gy_ref[...]
        value = gain * src[...]
        for k in range(7):
            moved = jnp.where(lane >= (1 << k), pltpu.roll(value, 1 << k, 1), 0.0)
            value = value + pw[k] * moved
        value = gain * value
        for k in range(7):
            moved = jnp.where(lane < 128 - (1 << k), pltpu.roll(value, 128 - (1 << k), 1), 0.0)
            value = value + pw[k] * moved
        dst[...] = value

    def sweep_x(src, dst, start, reverse):
        decay, gain = dec_ref[...], gain_ref[...]

        def step(i, total):
            for k in range(6):
                c = i * 6 + k
                if reverse:
                    c = NXB - 1 - c
                at = pl.ds(pl.multiple_of(c * LEV, LEV), LEV)
                total = decay * total + gain * src[at, :]
                dst[at, :] = total
            return total

        return lax.fori_loop(0, NXB // 6, step, start)

    def scan(values, reverse):
        sub = lax.broadcasted_iota(jnp.int32, (NDEV, 1), 0)
        factor = resp_ref[pl.ds(0, 1), :]
        for k in range(7):
            d = 1 << k
            if reverse:
                moved = jnp.where(sub < NDEV - d, pltpu.roll(values, NDEV - d, 0), 0.0)
            else:
                moved = jnp.where(sub >= d, pltpu.roll(values, d, 0), 0.0)
            values = values + factor * moved
            factor = factor * factor
        if reverse:
            return jnp.where(sub < NDEV - 1, pltpu.roll(values, NDEV - 1, 0), 0.0)
        return jnp.where(sub >= 1, pltpu.roll(values, 1, 0), 0.0)

    part = lax.rem(sub_i, 16)
    group_x = lev_i * 2 + sub_i // 16

    def exchange_one(turn, field):
        for z in range(LEV):
            tx1[turn, z // 2, pl.ds(z % 2 * NXB, NXB), :] = field[pl.ds(z, NXB, stride=LEV), :]

        def go(k, carry):
            to = lax.rem(part + k, 16)
            pltpu.make_async_remote_copy(
                src_ref=tx1.at[turn, to], dst_ref=ta.at[turn, part],
                send_sem=one_send.at[turn], recv_sem=one_recv.at[turn],
                device_id=(lev_i, sub_i - part + to), device_id_type=MESH,
            ).start()
            return carry

        lax.fori_loop(1, 16, go, 0)
        ta[turn, part] = tx1[turn, part]

    sub4 = lax.broadcasted_iota(jnp.int32, (1, 8, 1), 1) < 4
    to_lev = part // 4
    own_rows = lev_i == to_lev
    slot_two = pl.ds(pl.multiple_of(group_x * 384, 384), 384)

    def exchange_two(turn):
        fifteen = pl.ds(0, 15)
        wait_all(ta.at[turn, fifteen], ta.at[turn, fifteen], one_send.at[turn], one_recv.at[turn])
        lower = ta[turn, :, pl.ds(0, NXB), :].reshape(16 * NXB, 128).T.reshape(16, 8, 384)
        upper = ta[turn, :, pl.ds(NXB, NXB), :].reshape(16 * NXB, 128).T.reshape(16, 8, 384)
        even = jnp.where(sub4, lower, pltpu.roll(upper, 4, 1))
        odd = jnp.where(sub4, pltpu.roll(lower, 4, 1), upper)
        tx2[turn] = jnp.stack([even, odd], axis=1).reshape(NSUB, 8, 384)

        def send_rows(to):
            pltpu.make_async_remote_copy(
                src_ref=tx2.at[turn, to],
                dst_ref=tb.at[turn, lax.rem(part, 4), :, slot_two],
                send_sem=two_send.at[turn], recv_sem=two_recv.at[turn],
                device_id=(to_lev, to), device_id_type=MESH,
            ).start()

        def go(k, carry):
            send_rows(lax.rem(sub_i + k, NSUB))
            return carry

        lax.fori_loop(1, NSUB, go, 0)

        @pl.when(jnp.logical_not(own_rows))
        def _():
            send_rows(sub_i)

        @pl.when(own_rows)
        def _():
            tb[turn, lax.rem(part, 4), :, slot_two] = tx2[turn, sub_i]

    def finish_two(turn):
        @pl.when(own_rows)
        def _():
            most = tx2.at[turn, pl.ds(0, NSUB - 1)]
            wait_all(most, most, two_send.at[turn], two_recv.at[turn])

        @pl.when(jnp.logical_not(own_rows))
        def _():
            wait_all(tx2.at[turn], tx2.at[turn], two_send.at[turn], two_recv.at[turn])

    def covariance(turn, x_out, y_out):
        v[pl.ds(0, WROWS), :] = tacc[:, pl.ds(0, 128)] * sigma_ref[pl.ds(0, WROWS), :]
        v[pl.ds(WROWS, WROWS), :] = tacc[:, pl.ds(128, 128)] * sigma_ref[pl.ds(WROWS, WROWS), :]
        filter_z(v, ubuf, vbuf)
        filter_y(vbuf, v)
        zero = jnp.zeros((LEV, 128), F32)
        es[turn, :, 0, :] = sweep_x(v, ubuf, zero, False)
        es[turn, :, 1, :] = sweep_x(ubuf, vbuf, zero, True)
        es[turn, :, 2, :] = sweep_x(vbuf, ubuf, zero, False)
        es[turn, :, 3, :] = sweep_x(ubuf, vbuf, zero, True)

        def send_edges(k, carry):
            to = other(k)
            pltpu.make_async_remote_copy(
                src_ref=es.at[turn, lax.rem(to, NSUB)], dst_ref=el.at[turn, me],
                send_sem=edge_send.at[turn], recv_sem=edge_recv.at[turn],
                device_id=device(to), device_id_type=MESH,
            ).start()
            return carry

        lax.fori_loop(1, NDEV, send_edges, 0)
        el[turn, me] = es[turn, sub_i]
        if turn == 1:
            exchange_two(0)
        wait_all(el.at[turn, rest], el.at[turn, rest], edge_send.at[turn], edge_recv.at[turn])

        e1, e2 = el[turn, :, 0, :], el[turn, :, 1, :]
        e3, e4 = el[turn, :, 2, :], el[turn, :, 3, :]
        _, k1, k2, k3, k4, k5 = [resp_ref[pl.ds(i, 1), :] for i in range(6)]
        c1 = scan(e1, False)
        c2 = scan(e2 + k1 * c1, True)
        c3 = scan(e3 + k2 * c1 + k3 * c2, False)
        c4 = scan(e4 + k4 * c1 + k5 * c2 + k1 * c3, True)
        group = pl.ds(pl.multiple_of(lev_i * NSUB, NSUB), NSUB)
        for index, value in enumerate((c1, c2, c3, c4)):
            cs[...] = value
            cr[turn, :, index, :] = cs[group, :]

        def send_back(k, carry):
            to = lax.rem(sub_i + k, NSUB)
            pltpu.make_async_remote_copy(
                src_ref=cr.at[turn, to], dst_ref=cl.at[turn, sub_i],
                send_sem=back_send.at[turn], recv_sem=back_recv.at[turn],
                device_id=(lev_i, to), device_id_type=MESH,
            ).start()
            return carry

        lax.fori_loop(1, NSUB, send_back, 0)
        cl[turn, sub_i] = cr[turn, sub_i]
        back = pl.ds(0, NSUB - 1)
        wait_all(cl.at[turn, back], cl.at[turn, back], back_send.at[turn], back_recv.at[turn])
        sweep_x(v, ubuf, cl[turn, :, 0, :], False)
        sweep_x(ubuf, x_out, cl[turn, :, 1, :], True)
        exchange_one(turn, x_out)
        sweep_x(x_out, vbuf, cl[turn, :, 2, :], False)
        sweep_x(vbuf, ubuf, cl[turn, :, 3, :], True)
        filter_y(ubuf, vbuf)
        filter_z(vbuf, ubuf, v)
        y_out[...] = v[...] * sigma_ref[...]

    def share(turn, sums):
        row = jnp.zeros((1, 128), F32)
        for index, value in enumerate(sums):
            row = jnp.where(lane == index, value, row)
        sc_src[turn] = row

        def go(k, carry):
            pltpu.make_async_remote_copy(
                src_ref=sc_src.at[turn], dst_ref=sc_land.at[turn, me],
                send_sem=sc_send.at[turn], recv_sem=sc_recv.at[turn],
                device_id=device(other(k)), device_id_type=MESH,
            ).start()
            return carry

        lax.fori_loop(1, NDEV, go, 0)
        sc_land[turn, me] = row

    def collect(turn, count):
        wait_all(
            sc_land.at[turn, rest], sc_land.at[turn, rest], sc_send.at[turn], sc_recv.at[turn]
        )
        total = jnp.sum(sc_land[turn, :, 0, :], axis=0, keepdims=True)
        return [
            jnp.sum(jnp.where(lane == index, total, 0.0), axis=1, keepdims=True)
            for index in range(count)
        ]

    def dot(left, right):
        return jnp.sum(jnp.sum(left * right, axis=0, keepdims=True), axis=1, keepdims=True)

    zrow0, zrow1 = zs.at[pl.ds(0, 1)], zs.at[pl.ds(1, 1)]
    spread(innov_ref, True)
    covariance(0, x0, y0)
    observe(y0, zrow0)
    z0 = zrow0[...]
    share(0, [dot(x0[...], x0[...]), dot(z0, z0)])
    spread(zrow0, False)
    covariance(1, x1, y1)
    rr0, zz0 = collect(0, 2)
    alpha0 = rr0 / (rr0 + zz0)
    x1[...] = (1.0 - alpha0) * x0[...] - alpha0 * x1[...]
    y1[...] = (1.0 - alpha0) * y0[...] - alpha0 * y1[...]
    observe(y1, zrow1)
    z1 = zrow1[...]
    share(1, [dot(x1[...], x1[...]), dot(x1[...], x0[...]), dot(z1, z1), dot(z1, z0)])
    exchange_two(1)
    rr1, cross, zz1, zcross = collect(1, 4)
    beta = rr1 / rr0
    curvature = rr1 + zz1 + 2.0 * beta * (cross + zcross) + beta * beta * (rr0 + zz0)
    alpha1 = rr1 / curvature
    old = alpha0 + alpha1 * beta
    increment_ref[...] = old * y0[...] + alpha1 * y1[...]
    dep_ref[...] = old * z0 + alpha1 * z1 - innov_ref[...]
    finish_two(0)
    finish_two(1)
    control_ref[...] = (old + alpha1 * (1.0 - alpha0)) * tb[0] - (alpha1 * alpha0) * tb[1]


def body(
    length_x, length_y, length_z, sigma, obs_profile, obs_scale, innovation, obs_column, obs_count
):
    vmem = pl.BlockSpec(memory_space=pltpu.VMEM)
    field = pltpu.VMEM((CELLS, 128), F32)
    control, increment, departures = pl.pallas_call(
        kernel,
        out_shape=(
            jax.ShapeDtypeStruct((4, 8, NXB * NDEV), F32),
            jax.ShapeDtypeStruct((CELLS, 128), F32),
            jax.ShapeDtypeStruct((1, NOBS), F32),
        ),
        in_specs=[vmem] * 9,
        out_specs=(vmem,) * 3,
        scratch_shapes=[
            pltpu.VMEM((TILES, 128), F32),
            pltpu.VMEM((NDEV, 2, 128), F32),
            pltpu.VMEM((NDEV, 16, 128), BF16),
            pltpu.VMEM((NDEV, 16, 128), BF16),
            pltpu.VMEM((NDEV, 2, 128), F32),
            pltpu.VMEM((WROWS, NOBS), BF16),
            pltpu.VMEM((256, NOBS), BF16),
            pltpu.VMEM((1, NOBS), F32),
            pltpu.VMEM((LEV, 128), F32),
            pltpu.VMEM((LEV, 128), F32),
            pltpu.VMEM((LEV, 128), F32),
            pltpu.VMEM((8, 128), F32),
            pltpu.VMEM((7, CELLS, 128), F32),
            field,
            field,
            field,
            field,
            field,
            field,
            field,
            field,
            pltpu.VMEM((WROWS, 256), F32),
            pltpu.VMEM((256, WROWS), BF16),
            pltpu.VMEM((256, WROWS), BF16),
            pltpu.VMEM((2, NOBS), F32),
            pltpu.VMEM((2, LEV, 4, 128), F32),
            pltpu.VMEM((2, NDEV, 4, 128), F32),
            pltpu.VMEM((NDEV, 128), F32),
            pltpu.VMEM((2, NSUB, 4, 128), F32),
            pltpu.VMEM((2, LEV, 4, 128), F32),
            pltpu.VMEM((2, 1, 128), F32),
            pltpu.VMEM((2, NDEV, 1, 128), F32),
            pltpu.VMEM((2, 16, 2 * NXB, 128), F32),
            pltpu.VMEM((2, 16, 2 * NXB, 128), F32),
            pltpu.VMEM((2, NSUB, 8, 384), F32),
            pltpu.VMEM((2, 4, 8, NXB * NDEV), F32),
        ]
        + [pltpu.SemaphoreType.DMA((GROUPS,))] * 4
        + [pltpu.SemaphoreType.DMA((2,))] * 10,
        compiler_params=pltpu.CompilerParams(
            collective_id=0, has_side_effects=True, vmem_limit_bytes=56 << 20
        ),
    )(
        length_x, length_y, length_z, sigma.reshape(CELLS, 128), obs_profile,
        obs_scale.reshape(TILES, 128), innovation.reshape(TILES, 128),
        obs_column.reshape(TILES, 128), obs_count,
    )
    return (
        control.reshape(LEV // NLEV, NY // NSUB, NXB * NDEV),
        increment.reshape(NXB, LEV, NY),
        departures.reshape(NOBS),
    )


def solution(mesh):
    blocks = P(("lev", "sub"))
    placed = (
        P("lev", "sub"), blocks, blocks, blocks, P(None, ("lev", "sub")),
        blocks, blocks, blocks, P(),
    )
    return jax.shard_map(
        body,
        mesh=mesh,
        in_specs=placed,
        out_specs=(P("lev", "sub", None), blocks, blocks),
        check_vma=False,
    )
```

```python
import functools

import jax
import jax.numpy as jnp
from jax import lax
from jax.experimental import pallas as pl
from jax.experimental.pallas import tpu as pltpu
from jax.sharding import PartitionSpec as P

MESH = pl.DeviceIdType.MESH
F32 = jnp.float32
BF16 = jnp.bfloat16
NLEV = 4
NSUB = 32
NDEV = NLEV * NSUB
NXB = 24
LEV = 32
NY = 128
CAP = 64
CELLS = NXB * LEV
NOBS = NDEV * CAP
HALF = NXB // 2
WROWS = HALF * LEV
TILES = NOBS // 128
GROUPS = 4


def gain_of(decay):
    square = decay * decay
    below = jnp.sqrt(1.0 - square)
    return below * jnp.sqrt(below) / jnp.sqrt(jnp.sqrt(1.0 + square))


def chunked_loop(start, end, unroll, body):
    def step(i, carry):
        for k in range(unroll):
            body(i * unroll + k)
        return carry

    lax.fori_loop(start // unroll, end // unroll, step, 0)


def split(value):
    high = value.astype(BF16)
    return high, (value - high.astype(F32)).astype(BF16)


def kernel(
    lx_ref, ly_ref, lz_ref, sigma_ref, prof_ref, scale_ref, raw_ref, col_ref, count_ref,
    control_ref, increment_ref, dep_ref,
    live_ref, ms, ws, wl, ml, wide, rowhot, innov_ref, lenx_ref, dec_ref, gain_ref, resp_ref,
    pw, gy_ref, v, ubuf, vbuf, x0, y0, x1, y1, tacc, fth, ftl, zs,
    es, el, cs, cr, cl, sc_src, sc_land, tx1, ta, tx2, tb,
    meta_send, meta_recv, obs_send, obs_recv, edge_send, edge_recv, back_send, back_recv,
    sc_send, sc_recv, one_send, one_recv, two_send, two_recv,
):
    lev_i = lax.axis_index("lev")
    sub_i = lax.axis_index("sub")
    me = lev_i * NSUB + sub_i

    def device(index):
        return (index // NSUB, lax.rem(index, NSUB))

    def other(k):
        return lax.rem(me + k, NDEV)

    barrier = pltpu.get_barrier_semaphore()

    def greet(k, carry):
        pl.semaphore_signal(barrier, inc=1, device_id=device(other(k)), device_id_type=MESH)
        return carry

    lax.fori_loop(1, NDEV, greet, 0)

    lane = lax.broadcasted_iota(jnp.int32, (1, 128), 1)
    low_half = lane < CAP

    def wait_all(src, dst, send_sem, recv_sem):
        copy = pltpu.make_async_remote_copy(
            src_ref=src, dst_ref=dst, send_sem=send_sem, recv_sem=recv_sem,
            device_id=(lev_i, sub_i), device_id_type=MESH,
        )
        copy.wait_recv()
        copy.wait_send()

    rest = pl.ds(0, NDEV - 1)

    counts = jnp.broadcast_to(count_ref[pl.ds(me, 1), :], (TILES, 128))
    owner = lax.broadcasted_iota(jnp.int32, (TILES, 128), 1)
    tile = lax.broadcasted_iota(jnp.int32, (TILES, 128), 0)
    even_count = jnp.sum(jnp.where(owner == 2 * tile, counts, 0), axis=1, keepdims=True)
    odd_count = jnp.sum(jnp.where(owner == 2 * tile + 1, counts, 0), axis=1, keepdims=True)
    live = jnp.where(owner < CAP, owner, owner - CAP) < jnp.where(owner < CAP, even_count, odd_count)
    live_ref[...] = jnp.where(live, scale_ref[...], 0.0)
    innov_sent = jnp.where(live, raw_ref[...].astype(F32), 0.0)
    column = col_ref[...].astype(F32)
    row = jnp.floor((column + 0.5) * (1.0 / (NXB * NDEV)))
    first = (2 * tile + jnp.where(owner < CAP, 0, 1)) * NXB
    local = column - row * (NXB * NDEV) - first.astype(F32)
    half = jnp.where(local >= HALF, 1.0, 0.0)
    key_sent = (half * NY + row) * 16.0 + (local - HALF * half)
    even = jnp.where(low_half, innov_sent, pltpu.roll(key_sent, CAP, 1))
    odd = jnp.where(low_half, pltpu.roll(innov_sent, CAP, 1), key_sent)
    ms[:, 0, :] = jnp.stack([even, odd], axis=1).reshape(NDEV, 128)
    pick4 = (
        lax.broadcasted_iota(jnp.int32, (4, 128), 0)
        == lax.rem(lax.broadcasted_iota(jnp.int32, (4, 128), 1), 4)
    ).astype(F32)
    own = lax.dot_general(
        lx_ref[...], pick4, (((0,), (0,)), ((), ())),
        precision=lax.Precision.HIGHEST, preferred_element_type=F32,
    )
    own_at = lax.broadcasted_iota(jnp.int32, (8, 128), 1) // 4
    own = jnp.where(own_at == lax.broadcasted_iota(jnp.int32, (8, 128), 0), own, 0.0)
    ms[:, 1, :] = jnp.broadcast_to(jnp.sum(own, axis=0, keepdims=True), (NDEV, 128))

    def pack(i):
        at = pl.ds(pl.multiple_of(i * 128, 128), 128)
        w = prof_ref[:, at].astype(F32) * live_ref[pl.ds(i, 1), :]
        top, bottom = w[:16], w[16:]
        ws[2 * i] = jnp.where(low_half, top, pltpu.roll(bottom, CAP, 1)).astype(BF16)
        ws[2 * i + 1] = jnp.where(low_half, pltpu.roll(top, CAP, 1), bottom).astype(BF16)

    chunked_loop(0, TILES, 4, pack)
    pl.semaphore_wait(barrier, NDEV - 1)

    pair, core = me // 2, lax.rem(me, 2)
    PAIRS = TILES // GROUPS

    def send_meta(k, carry):
        to = other(k)
        pltpu.make_async_remote_copy(
            src_ref=ms.at[to], dst_ref=ml.at[me], send_sem=meta_send.at[0],
            recv_sem=meta_recv.at[0], device_id=device(to), device_id_type=MESH,
        ).start()
        return carry

    def send_block(kp, to_core):
        to = 2 * lax.rem(pair + kp, TILES) + to_core
        group = kp // PAIRS
        pltpu.make_async_remote_copy(
            src_ref=ws.at[to], dst_ref=wl.at[me],
            send_sem=obs_send.at[group], recv_sem=obs_recv.at[group],
            device_id=device(to), device_id_type=MESH,
        ).start()

    def send_pair(kp, carry):
        send_block(kp, core)
        send_block(kp, 1 - core)
        return carry

    lax.fori_loop(1, NDEV, send_meta, 0)
    send_block(0, 1 - core)
    lax.fori_loop(1, TILES, send_pair, 0)
    ml[me] = ms[me]
    wl[me] = ws[me]

    decay_y = jnp.exp(-1.0 / ly_ref[...])
    gain_y = gain_of(decay_y).T
    decay_y = decay_y.T
    for c in range(NXB):
        rows = pl.ds(c * LEV, LEV)
        gy_ref[rows, :] = jnp.broadcast_to(gain_y[:, c:c + 1], (LEV, 128))
        power = jnp.broadcast_to(decay_y[:, c:c + 1], (LEV, 128))
        for k in range(7):
            pw[k, rows, :] = power
            power = power * power
    decay_z = jnp.exp(-1.0 / lz_ref[...])
    gain_z = gain_of(decay_z)

    wait_all(ms.at[rest], ml.at[rest], meta_send.at[0], meta_recv.at[0])

    lengths = ml[:, 1, :]
    k_id = lax.broadcasted_iota(jnp.int32, (128, 128), 0)
    y_id = lax.broadcasted_iota(jnp.int32, (128, 128), 1)
    mine = (lax.rem(k_id, NSUB) == y_id // 4).astype(F32)
    for row in range(8):
        pick = (k_id == row * 4 + lax.rem(y_id, 4)).astype(F32)
        spread_row = jnp.dot(
            lengths, pick, precision=lax.Precision.HIGHEST, preferred_element_type=F32
        )
        rows = jnp.sum((spread_row * mine).reshape(NLEV, NSUB, 128), axis=1)
        lenx_ref[pl.ds(row, NLEV, stride=8), :] = rows
    decay_x = jnp.exp(-1.0 / lenx_ref[...])
    gain_x = gain_of(decay_x)
    dec_ref[...] = decay_x
    gain_ref[...] = gain_x

    place = lax.broadcasted_iota(jnp.int32, (256, 128), 0).astype(F32).astype(BF16)

    def widen(kp):
        i = lax.rem(pair - kp + TILES, TILES)
        at = pl.ds(pl.multiple_of(i * 128, 128), 128)
        even, odd = wl[2 * i].astype(F32), wl[2 * i + 1].astype(F32)
        low = jnp.where(low_half, even, pltpu.roll(odd, CAP, 1))
        high = jnp.where(low_half, pltpu.roll(even, CAP, 1), odd)
        w = jnp.concatenate([low, high], axis=0).astype(BF16)
        m_even, m_odd = ml[2 * i, pl.ds(0, 1), :], ml[2 * i + 1, pl.ds(0, 1), :]
        innov_ref[:, at] = jnp.where(low_half, m_even, pltpu.roll(m_odd, CAP, 1))
        key = jnp.where(low_half, pltpu.roll(m_even, CAP, 1), m_odd)
        spot = jnp.floor(key * (1.0 / 16.0))
        column = jnp.broadcast_to(key - 16.0 * spot, (LEV, 128)).astype(BF16)
        for c in range(HALF):
            wide[pl.ds(c * LEV, LEV), at] = jnp.where(column == c, w, jnp.zeros_like(w))
        spot = jnp.broadcast_to(spot, (256, 128)).astype(BF16)
        rowhot[:, at] = jnp.where(place == spot, jnp.ones_like(place), jnp.zeros_like(place))

    for group in range(GROUPS):
        blocks = pl.ds(0, 2 * PAIRS - (group == 0))
        wait_all(ws.at[blocks], wl.at[blocks], obs_send.at[group], obs_recv.at[group])
        chunked_loop(group * PAIRS, (group + 1) * PAIRS, 4, widen)

    def answer():
        level = pl.ds(sub_i, 1)
        a = dec_ref[level, :]
        g = gain_ref[level, :]
        up = [a]
        for _ in range(NXB - 1):
            up.append(up[-1] * a)

        def sweep(values):
            total = jnp.zeros_like(a)
            out = []
            for value in values:
                total = a * total + g * value
                out.append(total)
            return out

        block_decay = up[-1]
        p1 = sweep(up[::-1])[::-1]
        q1 = sweep(p1)
        q2 = sweep(up[::-1])
        r1 = sweep(q1[::-1])
        r2 = sweep(q2[::-1])
        for index, value in enumerate((block_decay, p1[0], q1[-1], q2[-1], r1[-1], r2[-1])):
            resp_ref[pl.ds(index, 1), :] = value

    CHUNK = 2048

    def spread(source, exact):
        tacc[...] = jnp.zeros_like(tacc)

        def step(i, carry):
            at = pl.ds(pl.multiple_of(i * CHUNK, CHUNK), CHUNK)
            hot = rowhot[:, at]
            parts = split(source[:, at])
            if exact:
                parts = parts[:1]
            total = tacc[...]
            for part in parts:
                total += lax.dot_general(
                    wide[:, at], hot * part, (((1,), (1,)), ((), ())),
                    preferred_element_type=F32,
                )
            tacc[...] = total
            return carry

        lax.fori_loop(0, NOBS // CHUNK, step, 0)

    def observe(field, out):
        side = jnp.concatenate([field[pl.ds(0, WROWS), :], field[pl.ds(WROWS, WROWS), :]], axis=1)
        fth[...], ftl[...] = split(side.T)

        def step(i, carry):
            at = pl.ds(pl.multiple_of(i * CHUNK, CHUNK), CHUNK)
            w = wide[:, at]
            got = jnp.dot(fth[...], w, preferred_element_type=F32)
            got += jnp.dot(ftl[...], w, preferred_element_type=F32)
            out[:, at] = jnp.sum(got * rowhot[:, at].astype(F32), axis=0, keepdims=True)
            return carry

        lax.fori_loop(0, NOBS // CHUNK, step, 0)

    def filter_z(src, mid, dst):
        def row(z):
            return pl.ds(z, NXB, stride=LEV)

        total = jnp.zeros((NXB, 128), F32)
        for z in range(LEV):
            total = decay_z * total + gain_z * src[row(z), :]
            mid[row(z), :] = total
        total = jnp.zeros((NXB, 128), F32)
        for z in range(LEV - 1, -1, -1):
            total = decay_z * total + gain_z * mid[row(z), :]
            dst[row(z), :] = total

    def filter_y(src, dst):
        gain = gy_ref[...]
        value = gain * src[...]
        for k in range(7):
            moved = jnp.where(lane >= (1 << k), pltpu.roll(value, 1 << k, 1), 0.0)
            value = value + pw[k] * moved
        value = gain * value
        for k in range(7):
            moved = jnp.where(lane < 128 - (1 << k), pltpu.roll(value, 128 - (1 << k), 1), 0.0)
            value = value + pw[k] * moved
        dst[...] = value

    def sweep_x(src, dst, start, reverse):
        decay, gain = dec_ref[...], gain_ref[...]

        def step(i, total):
            for k in range(6):
                c = i * 6 + k
                if reverse:
                    c = NXB - 1 - c
                at = pl.ds(pl.multiple_of(c * LEV, LEV), LEV)
                total = decay * total + gain * src[at, :]
                dst[at, :] = total
            return total

        return lax.fori_loop(0, NXB // 6, step, start)

    def scan(values, reverse):
        sub = lax.broadcasted_iota(jnp.int32, (NDEV, 1), 0)
        factor = resp_ref[pl.ds(0, 1), :]
        for k in range(7):
            d = 1 << k
            if reverse:
                moved = jnp.where(sub < NDEV - d, pltpu.roll(values, NDEV - d, 0), 0.0)
            else:
                moved = jnp.where(sub >= d, pltpu.roll(values, d, 0), 0.0)
            values = values + factor * moved
            factor = factor * factor
        if reverse:
            return jnp.where(sub < NDEV - 1, pltpu.roll(values, NDEV - 1, 0), 0.0)
        return jnp.where(sub >= 1, pltpu.roll(values, 1, 0), 0.0)

    part = lax.rem(sub_i, 16)
    group_x = lev_i * 2 + sub_i // 16

    def exchange_one(turn, field):
        for z in range(LEV):
            group, inner = z // 8, z % 8
            at = pl.ds(group % 2 * NXB, NXB)
            tx1[turn, inner * 2 + group // 2, at, :] = field[pl.ds(z, NXB, stride=LEV), :]

        def go(k, carry):
            to = lax.rem(part + k, 16)
            pltpu.make_async_remote_copy(
                src_ref=tx1.at[turn, to], dst_ref=ta.at[turn, part],
                send_sem=one_send.at[turn], recv_sem=one_recv.at[turn],
                device_id=(lev_i, sub_i - part + to), device_id_type=MESH,
            ).start()
            return carry

        lax.fori_loop(1, 16, go, 0)
        ta[turn, part] = tx1[turn, part]

    inner_lev, first_lev = part // 2, lax.rem(part, 2) * 2
    own_rows = lev_i // 2 == lax.rem(part, 2)
    slot_two = pl.ds(pl.multiple_of(group_x * 384, 384), 384)

    def exchange_two(turn):
        fifteen = pl.ds(0, 15)
        wait_all(ta.at[turn, fifteen], ta.at[turn, fifteen], one_send.at[turn], one_recv.at[turn])
        for which in range(2):
            block = ta[turn, :, pl.ds(which * NXB, NXB), :].reshape(16 * NXB, 128)
            tx2[turn, pl.ds(which * NSUB, NSUB)] = block.T.reshape(NSUB, 4, 384)

        def send_rows(which, to):
            pltpu.make_async_remote_copy(
                src_ref=tx2.at[turn, which * NSUB + to], dst_ref=tb.at[turn, inner_lev, :, slot_two],
                send_sem=two_send.at[turn], recv_sem=two_recv.at[turn],
                device_id=(first_lev + which, to), device_id_type=MESH,
            ).start()

        def go(k, carry):
            to = lax.rem(sub_i + k, NSUB)
            send_rows(0, to)
            send_rows(1, to)
            return carry

        lax.fori_loop(1, NSUB, go, 0)

        @pl.when(jnp.logical_not(own_rows))
        def _():
            send_rows(0, sub_i)
            send_rows(1, sub_i)

        @pl.when(own_rows)
        def _():
            mine = lax.rem(lev_i, 2)
            send_rows(1 - mine, sub_i)
            tb[turn, inner_lev, :, slot_two] = tx2[turn, mine * NSUB + sub_i]

    def finish_two(turn):
        @pl.when(own_rows)
        def _():
            most = tx2.at[turn, pl.ds(0, 2 * NSUB - 1)]
            wait_all(most, most, two_send.at[turn], two_recv.at[turn])

        @pl.when(jnp.logical_not(own_rows))
        def _():
            wait_all(tx2.at[turn], tx2.at[turn], two_send.at[turn], two_recv.at[turn])

    def covariance(turn, x_out, y_out):
        v[pl.ds(0, WROWS), :] = tacc[:, pl.ds(0, 128)] * sigma_ref[pl.ds(0, WROWS), :]
        v[pl.ds(WROWS, WROWS), :] = tacc[:, pl.ds(128, 128)] * sigma_ref[pl.ds(WROWS, WROWS), :]
        filter_z(v, ubuf, vbuf)
        filter_y(vbuf, v)
        zero = jnp.zeros((LEV, 128), F32)
        es[turn, :, 0, :] = sweep_x(v, ubuf, zero, False)
        es[turn, :, 1, :] = sweep_x(ubuf, vbuf, zero, True)
        es[turn, :, 2, :] = sweep_x(vbuf, ubuf, zero, False)
        es[turn, :, 3, :] = sweep_x(ubuf, vbuf, zero, True)

        def send_edges(k, carry):
            to = other(k)
            pltpu.make_async_remote_copy(
                src_ref=es.at[turn, lax.rem(to, NSUB)], dst_ref=el.at[turn, me],
                send_sem=edge_send.at[turn], recv_sem=edge_recv.at[turn],
                device_id=device(to), device_id_type=MESH,
            ).start()
            return carry

        lax.fori_loop(1, NDEV, send_edges, 0)
        el[turn, me] = es[turn, sub_i]
        if turn == 0:
            answer()
        wait_all(el.at[turn, rest], el.at[turn, rest], edge_send.at[turn], edge_recv.at[turn])

        e1, e2 = el[turn, :, 0, :], el[turn, :, 1, :]
        e3, e4 = el[turn, :, 2, :], el[turn, :, 3, :]
        _, k1, k2, k3, k4, k5 = [resp_ref[pl.ds(i, 1), :] for i in range(6)]
        c1 = scan(e1, False)
        c2 = scan(e2 + k1 * c1, True)
        c3 = scan(e3 + k2 * c1 + k3 * c2, False)
        c4 = scan(e4 + k4 * c1 + k5 * c2 + k1 * c3, True)
        group = pl.ds(pl.multiple_of(lev_i * NSUB, NSUB), NSUB)
        for index, value in enumerate((c1, c2, c3, c4)):
            cs[...] = value
            cr[turn, :, index, :] = cs[group, :]

        def send_back(k, carry):
            to = lax.rem(sub_i + k, NSUB)
            pltpu.make_async_remote_copy(
                src_ref=cr.at[turn, to], dst_ref=cl.at[turn, sub_i],
                send_sem=back_send.at[turn], recv_sem=back_recv.at[turn],
                device_id=(lev_i, to), device_id_type=MESH,
            ).start()
            return carry

        lax.fori_loop(1, NSUB, send_back, 0)
        cl[turn, sub_i] = cr[turn, sub_i]
        back = pl.ds(0, NSUB - 1)
        wait_all(cl.at[turn, back], cl.at[turn, back], back_send.at[turn], back_recv.at[turn])
        sweep_x(v, ubuf, cl[turn, :, 0, :], False)
        sweep_x(ubuf, x_out, cl[turn, :, 1, :], True)
        exchange_one(turn, x_out)
        sweep_x(x_out, vbuf, cl[turn, :, 2, :], False)
        sweep_x(vbuf, ubuf, cl[turn, :, 3, :], True)
        filter_y(ubuf, vbuf)
        filter_z(vbuf, ubuf, v)
        y_out[...] = v[...] * sigma_ref[...]

    def share(turn, sums):
        row = jnp.zeros((1, 128), F32)
        for index, value in enumerate(sums):
            row = jnp.where(lane == index, value, row)
        sc_src[turn] = row

        def go(k, carry):
            pltpu.make_async_remote_copy(
                src_ref=sc_src.at[turn], dst_ref=sc_land.at[turn, me],
                send_sem=sc_send.at[turn], recv_sem=sc_recv.at[turn],
                device_id=device(other(k)), device_id_type=MESH,
            ).start()
            return carry

        lax.fori_loop(1, NDEV, go, 0)
        sc_land[turn, me] = row

    def collect(turn, count):
        wait_all(
            sc_land.at[turn, rest], sc_land.at[turn, rest], sc_send.at[turn], sc_recv.at[turn]
        )
        total = jnp.sum(sc_land[turn, :, 0, :], axis=0, keepdims=True)
        return [
            jnp.sum(jnp.where(lane == index, total, 0.0), axis=1, keepdims=True)
            for index in range(count)
        ]

    def dot(left, right):
        return jnp.sum(jnp.sum(left * right, axis=0, keepdims=True), axis=1, keepdims=True)

    zrow0, zrow1 = zs.at[pl.ds(0, 1)], zs.at[pl.ds(1, 1)]
    spread(innov_ref, True)
    covariance(0, x0, y0)
    observe(y0, zrow0)
    z0 = zrow0[...]
    share(0, [dot(x0[...], x0[...]), dot(z0, z0)])
    exchange_two(0)
    spread(zrow0, False)
    covariance(1, x1, y1)
    rr0, zz0 = collect(0, 2)
    alpha0 = rr0 / (rr0 + zz0)
    x1[...] = (1.0 - alpha0) * x0[...] - alpha0 * x1[...]
    y1[...] = (1.0 - alpha0) * y0[...] - alpha0 * y1[...]
    observe(y1, zrow1)
    z1 = zrow1[...]
    share(1, [dot(x1[...], x1[...]), dot(x1[...], x0[...]), dot(z1, z1), dot(z1, z0)])
    exchange_two(1)
    rr1, cross, zz1, zcross = collect(1, 4)
    beta = rr1 / rr0
    curvature = rr1 + zz1 + 2.0 * beta * (cross + zcross) + beta * beta * (rr0 + zz0)
    alpha1 = rr1 / curvature
    old = alpha0 + alpha1 * beta
    increment_ref[...] = old * y0[...] + alpha1 * y1[...]
    dep_ref[...] = old * z0 + alpha1 * z1 - innov_ref[...]
    finish_two(0)
    finish_two(1)
    control_ref[...] = (old + alpha1 * (1.0 - alpha0)) * tb[0] - (alpha1 * alpha0) * tb[1]


def body(
    length_x, length_y, length_z, sigma, obs_profile, obs_scale, innovation, obs_column, obs_count
):
    vmem = pl.BlockSpec(memory_space=pltpu.VMEM)
    field = pltpu.VMEM((CELLS, 128), F32)
    control, increment, departures = pl.pallas_call(
        kernel,
        out_shape=(
            jax.ShapeDtypeStruct((8, 4, NXB * NDEV), F32),
            jax.ShapeDtypeStruct((CELLS, 128), F32),
            jax.ShapeDtypeStruct((1, NOBS), F32),
        ),
        in_specs=[vmem] * 9,
        out_specs=(vmem,) * 3,
        scratch_shapes=[
            pltpu.VMEM((TILES, 128), F32),
            pltpu.VMEM((NDEV, 2, 128), F32),
            pltpu.VMEM((NDEV, 16, 128), BF16),
            pltpu.VMEM((NDEV, 16, 128), BF16),
            pltpu.VMEM((NDEV, 2, 128), F32),
            pltpu.VMEM((WROWS, NOBS), BF16),
            pltpu.VMEM((256, NOBS), BF16),
            pltpu.VMEM((1, NOBS), F32),
            pltpu.VMEM((LEV, 128), F32),
            pltpu.VMEM((LEV, 128), F32),
            pltpu.VMEM((LEV, 128), F32),
            pltpu.VMEM((8, 128), F32),
            pltpu.VMEM((7, CELLS, 128), F32),
            field,
            field,
            field,
            field,
            field,
            field,
            field,
            field,
            pltpu.VMEM((WROWS, 256), F32),
            pltpu.VMEM((256, WROWS), BF16),
            pltpu.VMEM((256, WROWS), BF16),
            pltpu.VMEM((2, NOBS), F32),
            pltpu.VMEM((2, LEV, 4, 128), F32),
            pltpu.VMEM((2, NDEV, 4, 128), F32),
            pltpu.VMEM((NDEV, 128), F32),
            pltpu.VMEM((2, NSUB, 4, 128), F32),
            pltpu.VMEM((2, LEV, 4, 128), F32),
            pltpu.VMEM((2, 1, 128), F32),
            pltpu.VMEM((2, NDEV, 1, 128), F32),
            pltpu.VMEM((2, 16, 2 * NXB, 128), F32),
            pltpu.VMEM((2, 16, 2 * NXB, 128), F32),
            pltpu.VMEM((2, 2 * NSUB, 4, 384), F32),
            pltpu.VMEM((2, 8, 4, NXB * NDEV), F32),
        ]
        + [pltpu.SemaphoreType.DMA((1,))] * 2
        + [pltpu.SemaphoreType.DMA((GROUPS,))] * 2
        + [pltpu.SemaphoreType.DMA((2,))] * 10,
        compiler_params=pltpu.CompilerParams(
            collective_id=0, has_side_effects=True, vmem_limit_bytes=56 << 20
        ),
    )(
        length_x.T, length_y, length_z, sigma.reshape(CELLS, 128), obs_profile,
        obs_scale.reshape(TILES, 128), innovation.reshape(TILES, 128),
        obs_column.reshape(TILES, 128), obs_count,
    )
    return (
        control,
        increment.reshape(NXB, LEV, NY),
        departures.reshape(NOBS),
    )


def solution(mesh):
    blocks = P(("lev", "sub"))
    placed = (
        P("lev", "sub"), blocks, blocks, blocks, P(None, ("lev", "sub")),
        blocks, blocks, blocks, P(),
    )
    return jax.shard_map(
        body,
        mesh=mesh,
        in_specs=placed,
        out_specs=(P("lev", "sub", None), blocks, blocks),
        check_vma=False,
    )
```

```python
import functools

import jax
import jax.numpy as jnp
from jax import lax
from jax.experimental import pallas as pl
from jax.experimental.pallas import tpu as pltpu
from jax.sharding import PartitionSpec as P

MESH = pl.DeviceIdType.MESH
F32 = jnp.float32
BF16 = jnp.bfloat16
NLEV = 4
NSUB = 32
NDEV = NLEV * NSUB
NXB = 24
LEV = 32
NY = 128
CAP = 64
CELLS = NXB * LEV
NOBS = NDEV * CAP
HALF = NXB // 2
WROWS = HALF * LEV
TILES = NOBS // 128
GROUPS = 4


def gain_of(decay):
    square = decay * decay
    below = jnp.sqrt(1.0 - square)
    return below * jnp.sqrt(below) / jnp.sqrt(jnp.sqrt(1.0 + square))


def chunked_loop(start, end, unroll, body):
    def step(i, carry):
        for k in range(unroll):
            body(i * unroll + k)
        return carry

    lax.fori_loop(start // unroll, end // unroll, step, 0)


def kernel(
    lx_ref, ly_ref, lz_ref, sigma_hbm, prof_hbm, scale_ref, raw_ref, col_ref, count_ref,
    control_ref, increment_ref, dep_ref,
    sigma_ref, prof_ref, live_ref, ms, ws, wl, ml, wide, rowhot, innov_ref, lenx_ref, dec_ref, gain_ref, resp_ref,
    pw, gy_ref, v, ubuf, vbuf, x0, y0, x1, y1, res, tacc, fth, zs,
    es, el, cs, cr, cl, sc_src, sc_land, tx1_0, ta_0, tx1_1, ta_1, tx2, tb, rows,
    meta_send, meta_recv, obs_send, obs_recv, edge_send, edge_recv, back_send, back_recv,
    sc_send, sc_recv, one_send, one_recv, two_send, two_recv, load_sem,
):
    lev_i = lax.axis_index("lev")
    sub_i = lax.axis_index("sub")
    me = lev_i * NSUB + sub_i

    def device(index):
        return (index // NSUB, lax.rem(index, NSUB))

    def other(k):
        return lax.rem(me + k, NDEV)

    load_prof = pltpu.make_async_copy(prof_hbm, prof_ref, load_sem.at[0])
    load_sigma = pltpu.make_async_copy(sigma_hbm, sigma_ref, load_sem.at[1])
    load_prof.start()
    load_sigma.start()
    barrier = pltpu.get_barrier_semaphore()

    def greet(k, carry):
        pl.semaphore_signal(barrier, inc=1, device_id=device(other(k)), device_id_type=MESH)
        return carry

    lax.fori_loop(1, NDEV, greet, 0)

    lane = lax.broadcasted_iota(jnp.int32, (1, 128), 1)
    low_half = lane < CAP

    def wait_all(src, dst, send_sem, recv_sem):
        copy = pltpu.make_async_remote_copy(
            src_ref=src, dst_ref=dst, send_sem=send_sem, recv_sem=recv_sem,
            device_id=(lev_i, sub_i), device_id_type=MESH,
        )
        copy.wait_recv()
        copy.wait_send()

    rest = pl.ds(0, NDEV - 1)

    counts = jnp.broadcast_to(count_ref[pl.ds(me, 1), :], (TILES, 128))
    owner = lax.broadcasted_iota(jnp.int32, (TILES, 128), 1)
    tile = lax.broadcasted_iota(jnp.int32, (TILES, 128), 0)
    even_count = jnp.sum(jnp.where(owner == 2 * tile, counts, 0), axis=1, keepdims=True)
    odd_count = jnp.sum(jnp.where(owner == 2 * tile + 1, counts, 0), axis=1, keepdims=True)
    live = jnp.where(owner < CAP, owner, owner - CAP) < jnp.where(owner < CAP, even_count, odd_count)
    live_ref[...] = jnp.where(live, scale_ref[...], 0.0)
    innov_sent = jnp.where(live, raw_ref[...].astype(F32), 0.0)
    column = col_ref[...].astype(F32)
    row = jnp.floor((column + 0.5) * (1.0 / (NXB * NDEV)))
    first = (2 * tile + jnp.where(owner < CAP, 0, 1)) * NXB
    local = column - row * (NXB * NDEV) - first.astype(F32)
    half = jnp.where(local >= HALF, 1.0, 0.0)
    key_sent = (half * NY + row) * 16.0 + (local - HALF * half)
    even = jnp.where(low_half, innov_sent, pltpu.roll(key_sent, CAP, 1))
    odd = jnp.where(low_half, pltpu.roll(innov_sent, CAP, 1), key_sent)
    ms[:, 0, :] = jnp.stack([even, odd], axis=1).reshape(NDEV, 128)
    pick4 = (
        lax.broadcasted_iota(jnp.int32, (4, 128), 0)
        == lax.rem(lax.broadcasted_iota(jnp.int32, (4, 128), 1), 4)
    ).astype(F32)
    own = lax.dot_general(
        lx_ref[...], pick4, (((0,), (0,)), ((), ())),
        precision=lax.Precision.HIGHEST, preferred_element_type=F32,
    )
    own_at = lax.broadcasted_iota(jnp.int32, (8, 128), 1) // 4
    own = jnp.where(own_at == lax.broadcasted_iota(jnp.int32, (8, 128), 0), own, 0.0)
    ms[:, 1, :] = jnp.broadcast_to(jnp.sum(own, axis=0, keepdims=True), (NDEV, 128))

    def pack(i):
        at = pl.ds(pl.multiple_of(i * 128, 128), 128)
        w = prof_ref[:, at].astype(F32) * live_ref[pl.ds(i, 1), :]
        top, bottom = w[:16], w[16:]
        ws[2 * i] = jnp.where(low_half, top, pltpu.roll(bottom, CAP, 1)).astype(BF16)
        ws[2 * i + 1] = jnp.where(low_half, pltpu.roll(top, CAP, 1), bottom).astype(BF16)

    load_prof.wait()
    chunked_loop(0, TILES, 4, pack)
    pl.semaphore_wait(barrier, NDEV - 1)

    pair, core = me // 2, lax.rem(me, 2)
    PAIRS = TILES // GROUPS

    def send_meta(k, carry):
        to = other(k)
        pltpu.make_async_remote_copy(
            src_ref=ms.at[to], dst_ref=ml.at[me], send_sem=meta_send.at[0],
            recv_sem=meta_recv.at[0], device_id=device(to), device_id_type=MESH,
        ).start()
        return carry

    def send_block(kp, to_core):
        to = 2 * lax.rem(pair + kp, TILES) + to_core
        group = kp // PAIRS
        pltpu.make_async_remote_copy(
            src_ref=ws.at[to], dst_ref=wl.at[me],
            send_sem=obs_send.at[group], recv_sem=obs_recv.at[group],
            device_id=device(to), device_id_type=MESH,
        ).start()

    def send_pair(kp, carry):
        send_block(kp, core)
        send_block(kp, 1 - core)
        return carry

    lax.fori_loop(1, NDEV, send_meta, 0)
    send_block(0, 1 - core)
    lax.fori_loop(1, TILES, send_pair, 0)
    ml[me] = ms[me]
    wl[me] = ws[me]

    load_sigma.wait()
    decay_y = jnp.exp(-1.0 / ly_ref[...])
    gain_y = gain_of(decay_y).T
    decay_y = decay_y.T
    for c in range(NXB):
        cells = pl.ds(c * LEV, LEV)
        gy_ref[cells, :] = jnp.broadcast_to(gain_y[:, c:c + 1], (LEV, 128))
        power = jnp.broadcast_to(decay_y[:, c:c + 1], (LEV, 128))
        for k in range(7):
            pw[k, cells, :] = power
            power = power * power
    decay_z = jnp.exp(-1.0 / lz_ref[...])
    gain_z = gain_of(decay_z)

    wait_all(ms.at[rest], ml.at[rest], meta_send.at[0], meta_recv.at[0])

    lengths = ml[:, 1, :]
    k_id = lax.broadcasted_iota(jnp.int32, (128, 128), 0)
    y_id = lax.broadcasted_iota(jnp.int32, (128, 128), 1)
    mine = (lax.rem(k_id, NSUB) == y_id // 4).astype(F32)
    for row in range(8):
        pick = (k_id == row * 4 + lax.rem(y_id, 4)).astype(F32)
        spread_row = jnp.dot(
            lengths, pick, precision=lax.Precision.HIGHEST, preferred_element_type=F32
        )
        of_levels = jnp.sum((spread_row * mine).reshape(NLEV, NSUB, 128), axis=1)
        lenx_ref[pl.ds(row, NLEV, stride=8), :] = of_levels
    decay_x = jnp.exp(-1.0 / lenx_ref[...])
    gain_x = gain_of(decay_x)
    dec_ref[...] = decay_x
    gain_ref[...] = gain_x

    place = lax.broadcasted_iota(jnp.int32, (256, 128), 0).astype(F32).astype(BF16)

    def widen(kp):
        i = lax.rem(pair - kp + TILES, TILES)
        at = pl.ds(pl.multiple_of(i * 128, 128), 128)
        even, odd = wl[2 * i].astype(F32), wl[2 * i + 1].astype(F32)
        low = jnp.where(low_half, even, pltpu.roll(odd, CAP, 1))
        high = jnp.where(low_half, pltpu.roll(even, CAP, 1), odd)
        w = jnp.concatenate([low, high], axis=0).astype(BF16)
        m_even, m_odd = ml[2 * i, pl.ds(0, 1), :], ml[2 * i + 1, pl.ds(0, 1), :]
        innov_ref[:, at] = jnp.where(low_half, m_even, pltpu.roll(m_odd, CAP, 1))
        key = jnp.where(low_half, pltpu.roll(m_even, CAP, 1), m_odd)
        spot = jnp.floor(key * (1.0 / 16.0))
        column = jnp.broadcast_to(key - 16.0 * spot, (LEV, 128)).astype(BF16)
        for c in range(HALF):
            wide[pl.ds(c * LEV, LEV), at] = jnp.where(column == c, w, jnp.zeros_like(w))
        spot = jnp.broadcast_to(spot, (256, 128)).astype(BF16)
        rowhot[:, at] = jnp.where(place == spot, jnp.ones_like(place), jnp.zeros_like(place))

    for group in range(GROUPS):
        blocks = pl.ds(0, 2 * PAIRS - (group == 0))
        wait_all(ws.at[blocks], wl.at[blocks], obs_send.at[group], obs_recv.at[group])
        chunked_loop(group * PAIRS, (group + 1) * PAIRS, 4, widen)

    def answer():
        level = pl.ds(sub_i, 1)
        a = dec_ref[level, :]
        g = gain_ref[level, :]
        up = [a]
        for _ in range(NXB - 1):
            up.append(up[-1] * a)

        def sweep(values):
            total = jnp.zeros_like(a)
            out = []
            for value in values:
                total = a * total + g * value
                out.append(total)
            return out

        block_decay = up[-1]
        p1 = sweep(up[::-1])[::-1]
        q1 = sweep(p1)
        q2 = sweep(up[::-1])
        r1 = sweep(q1[::-1])
        r2 = sweep(q2[::-1])
        for index, value in enumerate((block_decay, p1[0], q1[-1], q2[-1], r1[-1], r2[-1])):
            resp_ref[pl.ds(index, 1), :] = value

    CHUNK = 4096

    def spread(source):
        tacc[...] = lax.dot_general(
            wide[...], rowhot[...] * source[...].astype(BF16), (((1,), (1,)), ((), ())),
            preferred_element_type=F32,
        )

    def observe(field, out):
        side = jnp.concatenate([field[pl.ds(0, WROWS), :], field[pl.ds(WROWS, WROWS), :]], axis=1)
        fth[...] = side.astype(BF16).T

        def step(i, carry):
            at = pl.ds(pl.multiple_of(i * CHUNK, CHUNK), CHUNK)
            w = wide[:, at]
            got = jnp.dot(fth[...], w, preferred_element_type=F32)
            out[:, at] = jnp.sum(got * rowhot[:, at].astype(F32), axis=0, keepdims=True)
            return carry

        lax.fori_loop(0, NOBS // CHUNK, step, 0)

    def filter_z(src, mid, dst):
        def row(z):
            return pl.ds(z, NXB, stride=LEV)

        total = jnp.zeros((NXB, 128), F32)
        for z in range(LEV):
            total = decay_z * total + gain_z * src[row(z), :]
            mid[row(z), :] = total
        total = jnp.zeros((NXB, 128), F32)
        for z in range(LEV - 1, -1, -1):
            total = decay_z * total + gain_z * mid[row(z), :]
            dst[row(z), :] = total

    def filter_y(src, dst):
        gain = gy_ref[...]
        value = gain * src[...]
        for k in range(7):
            moved = jnp.where(lane >= (1 << k), pltpu.roll(value, 1 << k, 1), 0.0)
            value = value + pw[k] * moved
        value = gain * value
        for k in range(7):
            moved = jnp.where(lane < 128 - (1 << k), pltpu.roll(value, 128 - (1 << k), 1), 0.0)
            value = value + pw[k] * moved
        dst[...] = value

    def sweep_x(src, dst, start, reverse):
        decay, gain = dec_ref[...], gain_ref[...]

        def step(i, total):
            for k in range(6):
                c = i * 6 + k
                if reverse:
                    c = NXB - 1 - c
                at = pl.ds(pl.multiple_of(c * LEV, LEV), LEV)
                total = decay * total + gain * src[at, :]
                dst[at, :] = total
            return total

        return lax.fori_loop(0, NXB // 6, step, start)

    def scan(values, reverse):
        sub = lax.broadcasted_iota(jnp.int32, (NDEV, 1), 0)
        factor = resp_ref[pl.ds(0, 1), :]
        for k in range(7):
            d = 1 << k
            if reverse:
                moved = jnp.where(sub < NDEV - d, pltpu.roll(values, NDEV - d, 0), 0.0)
            else:
                moved = jnp.where(sub >= d, pltpu.roll(values, d, 0), 0.0)
            values = values + factor * moved
            factor = factor * factor
        if reverse:
            return jnp.where(sub < NDEV - 1, pltpu.roll(values, NDEV - 1, 0), 0.0)
        return jnp.where(sub >= 1, pltpu.roll(values, 1, 0), 0.0)

    part = lax.rem(sub_i, 16)
    group_x = lev_i * 2 + sub_i // 16

    tx1, ta = (tx1_0, tx1_1), (ta_0, ta_1)

    def exchange_one(turn, field):
        src, dst = tx1[turn], ta[turn]
        for which in range(2):
            for z in range(16):
                core_of, inner = z // 8, z % 8
                level = (core_of * 2 + which) * 8 + inner
                rows[which, inner * 2 + core_of] = field[pl.ds(level, NXB, stride=LEV), :]
        both = jnp.concatenate([rows[0], rows[1]], axis=1)
        src[...] = both.astype(src.dtype)

        def go(k, carry):
            to = lax.rem(part + k, 16)
            pltpu.make_async_remote_copy(
                src_ref=src.at[to], dst_ref=dst.at[part],
                send_sem=one_send.at[turn], recv_sem=one_recv.at[turn],
                device_id=(lev_i, sub_i - part + to), device_id_type=MESH,
            ).start()
            return carry

        lax.fori_loop(1, 16, go, 0)
        dst[part] = src[part]

    inner_lev, first_lev = part // 2, lax.rem(part, 2) * 2
    own_rows = lev_i // 2 == lax.rem(part, 2)
    slot_two = pl.ds(pl.multiple_of(group_x * 384, 384), 384)

    def exchange_two(turn):
        most = ta[turn].at[pl.ds(0, 15)]
        wait_all(most, most, one_send.at[turn], one_recv.at[turn])
        landed = ta[turn][...].astype(F32)
        for which in range(2):
            block = landed[:, which * NXB:(which + 1) * NXB, :].reshape(16 * NXB, 128)
            tx2[turn, pl.ds(which * NSUB, NSUB)] = block.T.reshape(NSUB, 4, 384)

        def send_rows(which, to):
            pltpu.make_async_remote_copy(
                src_ref=tx2.at[turn, which * NSUB + to], dst_ref=tb.at[turn, inner_lev, :, slot_two],
                send_sem=two_send.at[turn], recv_sem=two_recv.at[turn],
                device_id=(first_lev + which, to), device_id_type=MESH,
            ).start()

        def go(k, carry):
            to = lax.rem(sub_i + k, NSUB)
            send_rows(0, to)
            send_rows(1, to)
            return carry

        lax.fori_loop(1, NSUB, go, 0)

        @pl.when(jnp.logical_not(own_rows))
        def _():
            send_rows(0, sub_i)
            send_rows(1, sub_i)

        @pl.when(own_rows)
        def _():
            mine = lax.rem(lev_i, 2)
            send_rows(1 - mine, sub_i)
            tb[turn, inner_lev, :, slot_two] = tx2[turn, mine * NSUB + sub_i]

    def finish_two(turn):
        @pl.when(own_rows)
        def _():
            most = tx2.at[turn, pl.ds(0, 2 * NSUB - 1)]
            wait_all(most, most, two_send.at[turn], two_recv.at[turn])

        @pl.when(jnp.logical_not(own_rows))
        def _():
            wait_all(tx2.at[turn], tx2.at[turn], two_send.at[turn], two_recv.at[turn])

    def covariance(turn, x_out, y_out, after):
        v[pl.ds(0, WROWS), :] = tacc[:, pl.ds(0, 128)] * sigma_ref[pl.ds(0, WROWS), :]
        v[pl.ds(WROWS, WROWS), :] = tacc[:, pl.ds(128, 128)] * sigma_ref[pl.ds(WROWS, WROWS), :]
        filter_z(v, ubuf, vbuf)
        filter_y(vbuf, v)
        zero = jnp.zeros((LEV, 128), F32)
        es[turn, :, 0, :] = sweep_x(v, ubuf, zero, False)
        es[turn, :, 1, :] = sweep_x(ubuf, vbuf, zero, True)
        es[turn, :, 2, :] = sweep_x(vbuf, ubuf, zero, False)
        es[turn, :, 3, :] = sweep_x(ubuf, vbuf, zero, True)

        def send_edges(k, carry):
            to = other(k)
            pltpu.make_async_remote_copy(
                src_ref=es.at[turn, lax.rem(to, NSUB)], dst_ref=el.at[turn, me],
                send_sem=edge_send.at[turn], recv_sem=edge_recv.at[turn],
                device_id=device(to), device_id_type=MESH,
            ).start()
            return carry

        lax.fori_loop(1, NDEV, send_edges, 0)
        el[turn, me] = es[turn, sub_i]
        if turn == 0:
            answer()
        wait_all(el.at[turn, rest], el.at[turn, rest], edge_send.at[turn], edge_recv.at[turn])

        e1, e2 = el[turn, :, 0, :], el[turn, :, 1, :]
        e3, e4 = el[turn, :, 2, :], el[turn, :, 3, :]
        _, k1, k2, k3, k4, k5 = [resp_ref[pl.ds(i, 1), :] for i in range(6)]
        c1 = scan(e1, False)
        c2 = scan(e2 + k1 * c1, True)
        c3 = scan(e3 + k2 * c1 + k3 * c2, False)
        c4 = scan(e4 + k4 * c1 + k5 * c2 + k1 * c3, True)
        group = pl.ds(pl.multiple_of(lev_i * NSUB, NSUB), NSUB)
        for index, value in enumerate((c1, c2, c3, c4)):
            cs[...] = value
            cr[turn, :, index, :] = cs[group, :]

        def send_back(k, carry):
            to = lax.rem(sub_i + k, NSUB)
            pltpu.make_async_remote_copy(
                src_ref=cr.at[turn, to], dst_ref=cl.at[turn, sub_i],
                send_sem=back_send.at[turn], recv_sem=back_recv.at[turn],
                device_id=(lev_i, to), device_id_type=MESH,
            ).start()
            return carry

        lax.fori_loop(1, NSUB, send_back, 0)
        cl[turn, sub_i] = cr[turn, sub_i]
        back = pl.ds(0, NSUB - 1)
        wait_all(cl.at[turn, back], cl.at[turn, back], back_send.at[turn], back_recv.at[turn])
        sweep_x(v, ubuf, cl[turn, :, 0, :], False)
        sweep_x(ubuf, x_out, cl[turn, :, 1, :], True)
        after(turn, x_out)
        sweep_x(x_out, vbuf, cl[turn, :, 2, :], False)
        sweep_x(vbuf, ubuf, cl[turn, :, 3, :], True)
        filter_y(ubuf, vbuf)
        filter_z(vbuf, ubuf, v)
        y_out[...] = v[...] * sigma_ref[...]

    def share(turn, sums):
        row = jnp.zeros((1, 128), F32)
        for index, value in enumerate(sums):
            row = jnp.where(lane == index, value, row)
        sc_src[turn] = row

        def go(k, carry):
            pltpu.make_async_remote_copy(
                src_ref=sc_src.at[turn], dst_ref=sc_land.at[turn, me],
                send_sem=sc_send.at[turn], recv_sem=sc_recv.at[turn],
                device_id=device(other(k)), device_id_type=MESH,
            ).start()
            return carry

        lax.fori_loop(1, NDEV, go, 0)
        sc_land[turn, me] = row

    def collect(turn, count):
        wait_all(
            sc_land.at[turn, rest], sc_land.at[turn, rest], sc_send.at[turn], sc_recv.at[turn]
        )
        total = jnp.sum(sc_land[turn, :, 0, :], axis=0, keepdims=True)
        return [
            jnp.sum(jnp.where(lane == index, total, 0.0), axis=1, keepdims=True)
            for index in range(count)
        ]

    def dot(left, right):
        return jnp.sum(jnp.sum(left * right, axis=0, keepdims=True), axis=1, keepdims=True)

    zrow0, zrow1 = zs.at[pl.ds(0, 1)], zs.at[pl.ds(1, 1)]
    spread(innov_ref)
    covariance(0, x0, y0, exchange_one)
    observe(y0, zrow0)
    z0 = zrow0[...]
    share(0, [dot(x0[...], x0[...]), dot(z0, z0)])
    exchange_two(0)
    spread(zrow0)
    scalars = []

    def residual(turn, field):
        scalars.extend(collect(0, 2))
        rr0, zz0 = scalars
        alpha0 = rr0 / (rr0 + zz0)
        scalars.append(alpha0)
        res[...] = (1.0 - alpha0) * x0[...] - alpha0 * field[...]
        exchange_one(turn, res)

    covariance(1, x1, y1, residual)
    rr0, zz0, alpha0 = scalars
    y1[...] = (1.0 - alpha0) * y0[...] - alpha0 * y1[...]
    observe(y1, zrow1)
    z1 = zrow1[...]
    share(1, [dot(res[...], res[...]), dot(res[...], x0[...]), dot(z1, z1), dot(z1, z0)])
    exchange_two(1)
    rr1, cross, zz1, zcross = collect(1, 4)
    beta = rr1 / rr0
    curvature = rr1 + zz1 + 2.0 * beta * (cross + zcross) + beta * beta * (rr0 + zz0)
    alpha1 = rr1 / curvature
    old = alpha0 + alpha1 * beta
    increment_ref[...] = old * y0[...] + alpha1 * y1[...]
    dep_ref[...] = old * z0 + alpha1 * z1 - innov_ref[...]
    finish_two(0)
    finish_two(1)
    control_ref[...] = old * tb[0] + alpha1 * tb[1]


def hand_over(a_in, b_in, c_in, a_out, b_out, c_out):
    a_out[...] = a_in[...]
    b_out[...] = b_in[...]
    c_out[...] = c_in[...]


def body(
    length_x, length_y, length_z, sigma, obs_profile, obs_scale, innovation, obs_column, obs_count
):
    vmem = pl.BlockSpec(memory_space=pltpu.VMEM)
    field = pltpu.VMEM((CELLS, 128), F32)
    control, increment, departures = pl.pallas_call(
        kernel,
        out_shape=(
            jax.ShapeDtypeStruct((8, 4, NXB * NDEV), F32),
            jax.ShapeDtypeStruct((CELLS, 128), F32),
            jax.ShapeDtypeStruct((1, NOBS), F32),
        ),
        in_specs=[vmem] * 3 + [pl.BlockSpec(memory_space=pl.ANY)] * 2 + [vmem] * 4,
        out_specs=(vmem,) * 3,
        scratch_shapes=[
            field,
            pltpu.VMEM((LEV, NOBS), BF16),
            pltpu.VMEM((TILES, 128), F32),
            pltpu.VMEM((NDEV, 2, 128), F32),
            pltpu.VMEM((NDEV, 16, 128), BF16),
            pltpu.VMEM((NDEV, 16, 128), BF16),
            pltpu.VMEM((NDEV, 2, 128), F32),
            pltpu.VMEM((WROWS, NOBS), BF16),
            pltpu.VMEM((256, NOBS), BF16),
            pltpu.VMEM((1, NOBS), F32),
            pltpu.VMEM((LEV, 128), F32),
            pltpu.VMEM((LEV, 128), F32),
            pltpu.VMEM((LEV, 128), F32),
            pltpu.VMEM((8, 128), F32),
            pltpu.VMEM((7, CELLS, 128), F32),
            field,
            field,
            field,
            field,
            field,
            field,
            field,
            field,
            field,
            pltpu.VMEM((WROWS, 256), F32),
            pltpu.VMEM((256, WROWS), BF16),
            pltpu.VMEM((2, NOBS), F32),
            pltpu.VMEM((2, LEV, 4, 128), F32),
            pltpu.VMEM((2, NDEV, 4, 128), F32),
            pltpu.VMEM((NDEV, 128), F32),
            pltpu.VMEM((2, NSUB, 4, 128), F32),
            pltpu.VMEM((2, LEV, 4, 128), F32),
            pltpu.VMEM((2, 1, 128), F32),
            pltpu.VMEM((2, NDEV, 1, 128), F32),
            pltpu.VMEM((16, 2 * NXB, 128), F32),
            pltpu.VMEM((16, 2 * NXB, 128), F32),
            pltpu.VMEM((16, 2 * NXB, 128), BF16),
            pltpu.VMEM((16, 2 * NXB, 128), BF16),
            pltpu.VMEM((2, 2 * NSUB, 4, 384), F32),
            pltpu.VMEM((2, 8, 4, NXB * NDEV), F32),
            pltpu.VMEM((2, 16, NXB, 128), F32),
        ]
        + [pltpu.SemaphoreType.DMA((1,))] * 2
        + [pltpu.SemaphoreType.DMA((GROUPS,))] * 2
        + [pltpu.SemaphoreType.DMA((2,))] * 11,
        compiler_params=pltpu.CompilerParams(
            collective_id=0, has_side_effects=True, vmem_limit_bytes=56 << 20
        ),
    )(
        length_x.T, length_y, length_z, sigma.reshape(CELLS, 128), obs_profile,
        obs_scale.reshape(TILES, 128), innovation.reshape(TILES, 128),
        obs_column.reshape(TILES, 128), obs_count,
    )
    whole = pl.BlockSpec(memory_space=pltpu.VMEM)
    control, increment, departures = pl.pallas_call(
        hand_over,
        out_shape=(
            jax.ShapeDtypeStruct((8, 4, NXB * NDEV), F32),
            jax.ShapeDtypeStruct((CELLS, 128), F32),
            jax.ShapeDtypeStruct((1, NOBS), F32),
        ),
        in_specs=[whole] * 3,
        out_specs=(whole,) * 3,
    )(control, increment, departures)
    return (
        control,
        increment.reshape(NXB, LEV, NY),
        departures.reshape(NOBS),
    )


def solution(mesh):
    blocks = P(("lev", "sub"))
    placed = (
        P("lev", "sub"), blocks, blocks, blocks, P(None, ("lev", "sub")),
        blocks, blocks, blocks, P(),
    )
    return jax.shard_map(
        body,
        mesh=mesh,
        in_specs=placed,
        out_specs=(P("lev", "sub", None), blocks, blocks),
        check_vma=False,
    )
```

```python
import functools

import jax
import jax.numpy as jnp
from jax import lax
from jax.experimental import pallas as pl
from jax.experimental.pallas import tpu as pltpu
from jax.sharding import PartitionSpec as P

MESH = pl.DeviceIdType.MESH
F32 = jnp.float32
BF16 = jnp.bfloat16
NLEV = 4
NSUB = 32
NDEV = NLEV * NSUB
NXB = 24
LEV = 32
NY = 128
CAP = 64
CELLS = NXB * LEV
NOBS = NDEV * CAP
HALF = NXB // 2
WROWS = HALF * LEV
TILES = NOBS // 128
GROUPS = 4


def gain_of(decay):
    square = decay * decay
    below = jnp.sqrt(1.0 - square)
    return below * jnp.sqrt(below) / jnp.sqrt(jnp.sqrt(1.0 + square))


def chunked_loop(start, end, unroll, body):
    def step(i, carry):
        for k in range(unroll):
            body(i * unroll + k)
        return carry

    lax.fori_loop(start // unroll, end // unroll, step, 0)


def kernel(
    lx_ref, ly_ref, lz_ref, sigma_hbm, prof_hbm, scale_ref, raw_ref, col_ref, count_ref,
    control_ref, increment_ref, dep_ref,
    sigma_ref, prof_ref, live_ref, ms, ws, wl, ml, wide, rowhot, innov_ref, lenx_ref, dec_ref, gain_ref, resp_ref,
    pw, gy_ref, v, ubuf, vbuf, x0, y0, x1, y1, res, tacc, fth, zs,
    es, el, cs, cr, cl, sc_src, sc_land, tx1_0, ta_0, tx1_1, ta_1, tx2, tb, rows,
    meta_send, meta_recv, obs_send, obs_recv, edge_send, edge_recv, back_send, back_recv,
    sc_send, sc_recv, one_send, one_recv, two_send, two_recv, load_sem,
):
    lev_i = lax.axis_index("lev")
    sub_i = lax.axis_index("sub")
    me = lev_i * NSUB + sub_i

    def device(index):
        return (index // NSUB, lax.rem(index, NSUB))

    def other(k):
        return lax.rem(me + k, NDEV)

    load_prof = pltpu.make_async_copy(prof_hbm, prof_ref, load_sem.at[0])
    load_sigma = pltpu.make_async_copy(sigma_hbm, sigma_ref, load_sem.at[1])
    load_prof.start()
    load_sigma.start()
    barrier = pltpu.get_barrier_semaphore()

    def greet(k, carry):
        pl.semaphore_signal(barrier, inc=1, device_id=device(other(k)), device_id_type=MESH)
        return carry

    lax.fori_loop(1, NDEV, greet, 0)

    lane = lax.broadcasted_iota(jnp.int32, (1, 128), 1)
    low_half = lane < CAP

    def wait_all(src, dst, send_sem, recv_sem):
        copy = pltpu.make_async_remote_copy(
            src_ref=src, dst_ref=dst, send_sem=send_sem, recv_sem=recv_sem,
            device_id=(lev_i, sub_i), device_id_type=MESH,
        )
        copy.wait_recv()
        copy.wait_send()

    rest = pl.ds(0, NDEV - 1)

    counts = jnp.broadcast_to(count_ref[pl.ds(me, 1), :], (TILES, 128))
    owner = lax.broadcasted_iota(jnp.int32, (TILES, 128), 1)
    tile = lax.broadcasted_iota(jnp.int32, (TILES, 128), 0)
    even_count = jnp.sum(jnp.where(owner == 2 * tile, counts, 0), axis=1, keepdims=True)
    odd_count = jnp.sum(jnp.where(owner == 2 * tile + 1, counts, 0), axis=1, keepdims=True)
    live = jnp.where(owner < CAP, owner, owner - CAP) < jnp.where(owner < CAP, even_count, odd_count)
    live_ref[...] = jnp.where(live, scale_ref[...], 0.0)
    innov_sent = jnp.where(live, raw_ref[...].astype(F32), 0.0)
    column = col_ref[...].astype(F32)
    row = jnp.floor((column + 0.5) * (1.0 / (NXB * NDEV)))
    first = (2 * tile + jnp.where(owner < CAP, 0, 1)) * NXB
    local = column - row * (NXB * NDEV) - first.astype(F32)
    half = jnp.where(local >= HALF, 1.0, 0.0)
    key_sent = (half * NY + row) * 16.0 + (local - HALF * half)
    even = jnp.where(low_half, innov_sent, pltpu.roll(key_sent, CAP, 1))
    odd = jnp.where(low_half, pltpu.roll(innov_sent, CAP, 1), key_sent)
    ms[:, 0, :] = jnp.stack([even, odd], axis=1).reshape(NDEV, 128)
    pick4 = (
        lax.broadcasted_iota(jnp.int32, (4, 128), 0)
        == lax.rem(lax.broadcasted_iota(jnp.int32, (4, 128), 1), 4)
    ).astype(F32)
    own = lax.dot_general(
        lx_ref[...], pick4, (((0,), (0,)), ((), ())),
        precision=lax.Precision.HIGHEST, preferred_element_type=F32,
    )
    own_at = lax.broadcasted_iota(jnp.int32, (8, 128), 1) // 4
    own = jnp.where(own_at == lax.broadcasted_iota(jnp.int32, (8, 128), 0), own, 0.0)
    ms[:, 1, :] = jnp.broadcast_to(jnp.sum(own, axis=0, keepdims=True), (NDEV, 128))

    def pack(i):
        at = pl.ds(pl.multiple_of(i * 128, 128), 128)
        w = prof_ref[:, at].astype(F32) * live_ref[pl.ds(i, 1), :]
        top, bottom = w[:16], w[16:]
        ws[2 * i] = jnp.where(low_half, top, pltpu.roll(bottom, CAP, 1)).astype(BF16)
        ws[2 * i + 1] = jnp.where(low_half, pltpu.roll(top, CAP, 1), bottom).astype(BF16)

    load_prof.wait()
    chunked_loop(0, TILES, 4, pack)
    pl.semaphore_wait(barrier, NDEV - 1)

    pair, core = me // 2, lax.rem(me, 2)
    PAIRS = TILES // GROUPS

    def send_meta(k, carry):
        to = other(k)
        pltpu.make_async_remote_copy(
            src_ref=ms.at[to], dst_ref=ml.at[me], send_sem=meta_send.at[0],
            recv_sem=meta_recv.at[0], device_id=device(to), device_id_type=MESH,
        ).start()
        return carry

    def send_block(kp, to_core):
        to = 2 * lax.rem(pair + kp, TILES) + to_core
        group = kp // PAIRS
        pltpu.make_async_remote_copy(
            src_ref=ws.at[to], dst_ref=wl.at[me],
            send_sem=obs_send.at[group], recv_sem=obs_recv.at[group],
            device_id=device(to), device_id_type=MESH,
        ).start()

    def send_pair(kp, carry):
        send_block(kp, core)
        send_block(kp, 1 - core)
        return carry

    lax.fori_loop(1, NDEV, send_meta, 0)
    send_block(0, 1 - core)
    lax.fori_loop(1, TILES, send_pair, 0)
    ml[me] = ms[me]
    wl[me] = ws[me]

    load_sigma.wait()
    decay_y = jnp.exp(-1.0 / ly_ref[...])
    gain_y = gain_of(decay_y).T
    decay_y = decay_y.T
    for c in range(NXB):
        cells = pl.ds(c * LEV, LEV)
        gy_ref[cells, :] = jnp.broadcast_to(gain_y[:, c:c + 1], (LEV, 128))
        power = jnp.broadcast_to(decay_y[:, c:c + 1], (LEV, 128))
        for k in range(7):
            pw[k, cells, :] = power
            power = power * power
    decay_z = jnp.exp(-1.0 / lz_ref[...])
    gain_z = gain_of(decay_z)

    wait_all(ms.at[rest], ml.at[rest], meta_send.at[0], meta_recv.at[0])

    lengths = ml[:, 1, :]
    k_id = lax.broadcasted_iota(jnp.int32, (128, 128), 0)
    y_id = lax.broadcasted_iota(jnp.int32, (128, 128), 1)
    mine = (lax.rem(k_id, NSUB) == y_id // 4).astype(F32)
    for row in range(8):
        pick = (k_id == row * 4 + lax.rem(y_id, 4)).astype(F32)
        spread_row = jnp.dot(
            lengths, pick, precision=lax.Precision.HIGHEST, preferred_element_type=F32
        )
        of_levels = jnp.sum((spread_row * mine).reshape(NLEV, NSUB, 128), axis=1)
        lenx_ref[pl.ds(row, NLEV, stride=8), :] = of_levels
    decay_x = jnp.exp(-1.0 / lenx_ref[...])
    gain_x = gain_of(decay_x)
    dec_ref[...] = decay_x
    gain_ref[...] = gain_x

    place = lax.broadcasted_iota(jnp.int32, (256, 128), 0).astype(F32).astype(BF16)

    def widen(kp):
        i = lax.rem(pair - kp + TILES, TILES)
        at = pl.ds(pl.multiple_of(i * 128, 128), 128)
        even, odd = wl[2 * i].astype(F32), wl[2 * i + 1].astype(F32)
        low = jnp.where(low_half, even, pltpu.roll(odd, CAP, 1))
        high = jnp.where(low_half, pltpu.roll(even, CAP, 1), odd)
        w = jnp.concatenate([low, high], axis=0).astype(BF16)
        m_even, m_odd = ml[2 * i, pl.ds(0, 1), :], ml[2 * i + 1, pl.ds(0, 1), :]
        innov_ref[:, at] = jnp.where(low_half, m_even, pltpu.roll(m_odd, CAP, 1))
        key = jnp.where(low_half, pltpu.roll(m_even, CAP, 1), m_odd)
        spot = jnp.floor(key * (1.0 / 16.0))
        column = jnp.broadcast_to(key - 16.0 * spot, (LEV, 128)).astype(BF16)
        for c in range(HALF):
            wide[pl.ds(c * LEV, LEV), at] = jnp.where(column == c, w, jnp.zeros_like(w))
        spot = jnp.broadcast_to(spot, (256, 128)).astype(BF16)
        rowhot[:, at] = jnp.where(place == spot, jnp.ones_like(place), jnp.zeros_like(place))

    for group in range(GROUPS):
        blocks = pl.ds(0, 2 * PAIRS - (group == 0))
        wait_all(ws.at[blocks], wl.at[blocks], obs_send.at[group], obs_recv.at[group])
        chunked_loop(group * PAIRS, (group + 1) * PAIRS, 4, widen)

    def answer():
        level = pl.ds(sub_i, 1)
        a = dec_ref[level, :]
        g = gain_ref[level, :]
        up = [a]
        for _ in range(NXB - 1):
            up.append(up[-1] * a)

        def sweep(values):
            total = jnp.zeros_like(a)
            out = []
            for value in values:
                total = a * total + g * value
                out.append(total)
            return out

        block_decay = up[-1]
        p1 = sweep(up[::-1])[::-1]
        q1 = sweep(p1)
        q2 = sweep(up[::-1])
        r1 = sweep(q1[::-1])
        r2 = sweep(q2[::-1])
        for index, value in enumerate((block_decay, p1[0], q1[-1], q2[-1], r1[-1], r2[-1])):
            resp_ref[pl.ds(index, 1), :] = value

    CHUNK = 4096

    def spread(source):
        tacc[...] = lax.dot_general(
            wide[...], rowhot[...] * source[...].astype(BF16), (((1,), (1,)), ((), ())),
            preferred_element_type=F32,
        )

    def observe(field, out):
        side = jnp.concatenate([field[pl.ds(0, WROWS), :], field[pl.ds(WROWS, WROWS), :]], axis=1)
        fth[...] = side.astype(BF16).T

        def step(i, carry):
            at = pl.ds(pl.multiple_of(i * CHUNK, CHUNK), CHUNK)
            w = wide[:, at]
            got = jnp.dot(fth[...], w, preferred_element_type=F32)
            out[:, at] = jnp.sum(got * rowhot[:, at].astype(F32), axis=0, keepdims=True)
            return carry

        lax.fori_loop(0, NOBS // CHUNK, step, 0)

    def filter_z(src, mid, dst):
        def row(z):
            return pl.ds(z, NXB, stride=LEV)

        total = jnp.zeros((NXB, 128), F32)
        for z in range(LEV):
            total = decay_z * total + gain_z * src[row(z), :]
            mid[row(z), :] = total
        total = jnp.zeros((NXB, 128), F32)
        for z in range(LEV - 1, -1, -1):
            total = decay_z * total + gain_z * mid[row(z), :]
            dst[row(z), :] = total

    def filter_y(src, dst):
        gain = gy_ref[...]
        value = gain * src[...]
        for k in range(7):
            moved = jnp.where(lane >= (1 << k), pltpu.roll(value, 1 << k, 1), 0.0)
            value = value + pw[k] * moved
        value = gain * value
        for k in range(7):
            moved = jnp.where(lane < 128 - (1 << k), pltpu.roll(value, 128 - (1 << k), 1), 0.0)
            value = value + pw[k] * moved
        dst[...] = value

    def sweep_x(src, dst, start, reverse):
        decay, gain = dec_ref[...], gain_ref[...]

        def step(i, total):
            for k in range(6):
                c = i * 6 + k
                if reverse:
                    c = NXB - 1 - c
                at = pl.ds(pl.multiple_of(c * LEV, LEV), LEV)
                total = decay * total + gain * src[at, :]
                dst[at, :] = total
            return total

        return lax.fori_loop(0, NXB // 6, step, start)

    def scan(values, reverse):
        sub = lax.broadcasted_iota(jnp.int32, (NDEV, 1), 0)
        factor = resp_ref[pl.ds(0, 1), :]
        for k in range(7):
            d = 1 << k
            if reverse:
                moved = jnp.where(sub < NDEV - d, pltpu.roll(values, NDEV - d, 0), 0.0)
            else:
                moved = jnp.where(sub >= d, pltpu.roll(values, d, 0), 0.0)
            values = values + factor * moved
            factor = factor * factor
        if reverse:
            return jnp.where(sub < NDEV - 1, pltpu.roll(values, NDEV - 1, 0), 0.0)
        return jnp.where(sub >= 1, pltpu.roll(values, 1, 0), 0.0)

    part = lax.rem(sub_i, 16)
    group_x = lev_i * 2 + sub_i // 16

    tx1, ta = (tx1_0, tx1_1), (ta_0, ta_1)

    def exchange_one(turn, field):
        src, dst = tx1[turn], ta[turn]
        for which in range(2):
            for z in range(16):
                core_of, inner = z // 8, z % 8
                level = (core_of * 2 + which) * 8 + inner
                line = field[pl.ds(level, NXB, stride=LEV), :]
                if turn == 0:
                    src[inner * 2 + core_of, pl.ds(which * NXB, NXB), :] = line
                else:
                    rows[which, inner * 2 + core_of] = line
        if turn == 1:
            both = jnp.concatenate([rows[0], rows[1]], axis=1)
            src[...] = both.astype(src.dtype)

        def go(k, carry):
            to = lax.rem(part + k, 16)
            pltpu.make_async_remote_copy(
                src_ref=src.at[to], dst_ref=dst.at[part],
                send_sem=one_send.at[turn], recv_sem=one_recv.at[turn],
                device_id=(lev_i, sub_i - part + to), device_id_type=MESH,
            ).start()
            return carry

        lax.fori_loop(1, 16, go, 0)
        dst[part] = src[part]

    inner_lev, first_lev = part // 2, lax.rem(part, 2) * 2
    own_rows = lev_i // 2 == lax.rem(part, 2)
    slot_two = pl.ds(pl.multiple_of(group_x * 384, 384), 384)

    def exchange_two(turn):
        most = ta[turn].at[pl.ds(0, 15)]
        wait_all(most, most, one_send.at[turn], one_recv.at[turn])
        landed = ta[turn][...].astype(F32)
        for which in range(2):
            block = landed[:, which * NXB:(which + 1) * NXB, :].reshape(16 * NXB, 128)
            tx2[turn, pl.ds(which * NSUB, NSUB)] = block.T.reshape(NSUB, 4, 384)

        def send_rows(which, to):
            pltpu.make_async_remote_copy(
                src_ref=tx2.at[turn, which * NSUB + to], dst_ref=tb.at[turn, inner_lev, :, slot_two],
                send_sem=two_send.at[turn], recv_sem=two_recv.at[turn],
                device_id=(first_lev + which, to), device_id_type=MESH,
            ).start()

        def go(k, carry):
            to = lax.rem(sub_i + k, NSUB)
            send_rows(0, to)
            send_rows(1, to)
            return carry

        lax.fori_loop(1, NSUB, go, 0)

        @pl.when(jnp.logical_not(own_rows))
        def _():
            send_rows(0, sub_i)
            send_rows(1, sub_i)

        @pl.when(own_rows)
        def _():
            mine = lax.rem(lev_i, 2)
            send_rows(1 - mine, sub_i)
            tb[turn, inner_lev, :, slot_two] = tx2[turn, mine * NSUB + sub_i]

    def finish_two(turn):
        @pl.when(own_rows)
        def _():
            most = tx2.at[turn, pl.ds(0, 2 * NSUB - 1)]
            wait_all(most, most, two_send.at[turn], two_recv.at[turn])

        @pl.when(jnp.logical_not(own_rows))
        def _():
            wait_all(tx2.at[turn], tx2.at[turn], two_send.at[turn], two_recv.at[turn])

    def covariance(turn, x_out, y_out, after):
        v[pl.ds(0, WROWS), :] = tacc[:, pl.ds(0, 128)] * sigma_ref[pl.ds(0, WROWS), :]
        v[pl.ds(WROWS, WROWS), :] = tacc[:, pl.ds(128, 128)] * sigma_ref[pl.ds(WROWS, WROWS), :]
        filter_z(v, ubuf, vbuf)
        filter_y(vbuf, v)
        zero = jnp.zeros((LEV, 128), F32)
        es[turn, :, 0, :] = sweep_x(v, ubuf, zero, False)
        es[turn, :, 1, :] = sweep_x(ubuf, vbuf, zero, True)
        es[turn, :, 2, :] = sweep_x(vbuf, ubuf, zero, False)
        es[turn, :, 3, :] = sweep_x(ubuf, vbuf, zero, True)

        def send_edges(k, carry):
            to = other(k)
            pltpu.make_async_remote_copy(
                src_ref=es.at[turn, lax.rem(to, NSUB)], dst_ref=el.at[turn, me],
                send_sem=edge_send.at[turn], recv_sem=edge_recv.at[turn],
                device_id=device(to), device_id_type=MESH,
            ).start()
            return carry

        lax.fori_loop(1, NDEV, send_edges, 0)
        el[turn, me] = es[turn, sub_i]
        if turn == 0:
            answer()
        wait_all(el.at[turn, rest], el.at[turn, rest], edge_send.at[turn], edge_recv.at[turn])

        e1, e2 = el[turn, :, 0, :], el[turn, :, 1, :]
        e3, e4 = el[turn, :, 2, :], el[turn, :, 3, :]
        _, k1, k2, k3, k4, k5 = [resp_ref[pl.ds(i, 1), :] for i in range(6)]
        c1 = scan(e1, False)
        c2 = scan(e2 + k1 * c1, True)
        c3 = scan(e3 + k2 * c1 + k3 * c2, False)
        c4 = scan(e4 + k4 * c1 + k5 * c2 + k1 * c3, True)
        group = pl.ds(pl.multiple_of(lev_i * NSUB, NSUB), NSUB)
        for index, value in enumerate((c1, c2, c3, c4)):
            cs[...] = value
            cr[turn, :, index, :] = cs[group, :]

        def send_back(k, carry):
            to = lax.rem(sub_i + k, NSUB)
            pltpu.make_async_remote_copy(
                src_ref=cr.at[turn, to], dst_ref=cl.at[turn, sub_i],
                send_sem=back_send.at[turn], recv_sem=back_recv.at[turn],
                device_id=(lev_i, to), device_id_type=MESH,
            ).start()
            return carry

        lax.fori_loop(1, NSUB, send_back, 0)
        cl[turn, sub_i] = cr[turn, sub_i]
        back = pl.ds(0, NSUB - 1)
        wait_all(cl.at[turn, back], cl.at[turn, back], back_send.at[turn], back_recv.at[turn])
        sweep_x(v, ubuf, cl[turn, :, 0, :], False)
        sweep_x(ubuf, x_out, cl[turn, :, 1, :], True)
        after(turn, x_out)
        sweep_x(x_out, vbuf, cl[turn, :, 2, :], False)
        sweep_x(vbuf, ubuf, cl[turn, :, 3, :], True)
        filter_y(ubuf, vbuf)
        filter_z(vbuf, ubuf, v)
        y_out[...] = v[...] * sigma_ref[...]

    def share(turn, sums):
        row = jnp.zeros((1, 128), F32)
        for index, value in enumerate(sums):
            row = jnp.where(lane == index, value, row)
        sc_src[turn] = row

        def go(k, carry):
            pltpu.make_async_remote_copy(
                src_ref=sc_src.at[turn], dst_ref=sc_land.at[turn, me],
                send_sem=sc_send.at[turn], recv_sem=sc_recv.at[turn],
                device_id=device(other(k)), device_id_type=MESH,
            ).start()
            return carry

        lax.fori_loop(1, NDEV, go, 0)
        sc_land[turn, me] = row

    def collect(turn, count):
        wait_all(
            sc_land.at[turn, rest], sc_land.at[turn, rest], sc_send.at[turn], sc_recv.at[turn]
        )
        total = jnp.sum(sc_land[turn, :, 0, :], axis=0, keepdims=True)
        return [
            jnp.sum(jnp.where(lane == index, total, 0.0), axis=1, keepdims=True)
            for index in range(count)
        ]

    def dot(left, right):
        return jnp.sum(jnp.sum(left * right, axis=0, keepdims=True), axis=1, keepdims=True)

    zrow0, zrow1 = zs.at[pl.ds(0, 1)], zs.at[pl.ds(1, 1)]
    spread(innov_ref)
    covariance(0, x0, y0, exchange_one)
    observe(y0, zrow0)
    z0 = zrow0[...]
    share(0, [dot(x0[...], x0[...]), dot(z0, z0)])
    exchange_two(0)
    spread(zrow0)
    scalars = []

    def residual(turn, field):
        scalars.extend(collect(0, 2))
        rr0, zz0 = scalars
        alpha0 = rr0 / (rr0 + zz0)
        scalars.append(alpha0)
        res[...] = (1.0 - alpha0) * x0[...] - alpha0 * field[...]
        exchange_one(turn, res)

    covariance(1, x1, y1, residual)
    rr0, zz0, alpha0 = scalars
    y1[...] = (1.0 - alpha0) * y0[...] - alpha0 * y1[...]
    observe(y1, zrow1)
    z1 = zrow1[...]
    share(1, [dot(res[...], res[...]), dot(res[...], x0[...]), dot(z1, z1), dot(z1, z0)])
    exchange_two(1)
    rr1, cross, zz1, zcross = collect(1, 4)
    beta = rr1 / rr0
    curvature = rr1 + zz1 + 2.0 * beta * (cross + zcross) + beta * beta * (rr0 + zz0)
    alpha1 = rr1 / curvature
    old = alpha0 + alpha1 * beta
    increment_ref[...] = old * y0[...] + alpha1 * y1[...]
    dep_ref[...] = old * z0 + alpha1 * z1 - innov_ref[...]
    finish_two(0)
    finish_two(1)
    control_ref[...] = old * tb[0] + alpha1 * tb[1]


def hand_over(a_in, b_in, c_in, a_out, b_out, c_out):
    a_out[...] = a_in[...]
    b_out[...] = b_in[...]
    c_out[...] = c_in[...]


def body(
    length_x, length_y, length_z, sigma, obs_profile, obs_scale, innovation, obs_column, obs_count
):
    vmem = pl.BlockSpec(memory_space=pltpu.VMEM)
    field = pltpu.VMEM((CELLS, 128), F32)
    control, increment, departures = pl.pallas_call(
        kernel,
        out_shape=(
            jax.ShapeDtypeStruct((8, 4, NXB * NDEV), F32),
            jax.ShapeDtypeStruct((CELLS, 128), F32),
            jax.ShapeDtypeStruct((1, NOBS), F32),
        ),
        in_specs=[vmem] * 3 + [pl.BlockSpec(memory_space=pl.ANY)] * 2 + [vmem] * 4,
        out_specs=(vmem,) * 3,
        scratch_shapes=[
            field,
            pltpu.VMEM((LEV, NOBS), BF16),
            pltpu.VMEM((TILES, 128), F32),
            pltpu.VMEM((NDEV, 2, 128), F32),
            pltpu.VMEM((NDEV, 16, 128), BF16),
            pltpu.VMEM((NDEV, 16, 128), BF16),
            pltpu.VMEM((NDEV, 2, 128), F32),
            pltpu.VMEM((WROWS, NOBS), BF16),
            pltpu.VMEM((256, NOBS), BF16),
            pltpu.VMEM((1, NOBS), F32),
            pltpu.VMEM((LEV, 128), F32),
            pltpu.VMEM((LEV, 128), F32),
            pltpu.VMEM((LEV, 128), F32),
            pltpu.VMEM((8, 128), F32),
            pltpu.VMEM((7, CELLS, 128), F32),
            field,
            field,
            field,
            field,
            field,
            field,
            field,
            field,
            field,
            pltpu.VMEM((WROWS, 256), F32),
            pltpu.VMEM((256, WROWS), BF16),
            pltpu.VMEM((2, NOBS), F32),
            pltpu.VMEM((2, LEV, 4, 128), F32),
            pltpu.VMEM((2, NDEV, 4, 128), F32),
            pltpu.VMEM((NDEV, 128), F32),
            pltpu.VMEM((2, NSUB, 4, 128), F32),
            pltpu.VMEM((2, LEV, 4, 128), F32),
            pltpu.VMEM((2, 1, 128), F32),
            pltpu.VMEM((2, NDEV, 1, 128), F32),
            pltpu.VMEM((16, 2 * NXB, 128), F32),
            pltpu.VMEM((16, 2 * NXB, 128), F32),
            pltpu.VMEM((16, 2 * NXB, 128), BF16),
            pltpu.VMEM((16, 2 * NXB, 128), BF16),
            pltpu.VMEM((2, 2 * NSUB, 4, 384), F32),
            pltpu.VMEM((2, 8, 4, NXB * NDEV), F32),
            pltpu.VMEM((2, 16, NXB, 128), F32),
        ]
        + [pltpu.SemaphoreType.DMA((1,))] * 2
        + [pltpu.SemaphoreType.DMA((GROUPS,))] * 2
        + [pltpu.SemaphoreType.DMA((2,))] * 11,
        compiler_params=pltpu.CompilerParams(
            collective_id=0, has_side_effects=True, vmem_limit_bytes=56 << 20
        ),
    )(
        length_x.T, length_y, length_z, sigma.reshape(CELLS, 128), obs_profile,
        obs_scale.reshape(TILES, 128), innovation.reshape(TILES, 128),
        obs_column.reshape(TILES, 128), obs_count,
    )
    whole = pl.BlockSpec(memory_space=pltpu.VMEM)
    control, increment, departures = pl.pallas_call(
        hand_over,
        out_shape=(
            jax.ShapeDtypeStruct((8, 4, NXB * NDEV), F32),
            jax.ShapeDtypeStruct((CELLS, 128), F32),
            jax.ShapeDtypeStruct((1, NOBS), F32),
        ),
        in_specs=[whole] * 3,
        out_specs=(whole,) * 3,
    )(control, increment, departures)
    return (
        control,
        increment.reshape(NXB, LEV, NY),
        departures.reshape(NOBS),
    )


def solution(mesh):
    blocks = P(("lev", "sub"))
    placed = (
        P("lev", "sub"), blocks, blocks, blocks, P(None, ("lev", "sub")),
        blocks, blocks, blocks, P(),
    )
    return jax.shard_map(
        body,
        mesh=mesh,
        in_specs=placed,
        out_specs=(P("lev", "sub", None), blocks, blocks),
        check_vma=False,
    )
```
